128 devices in a mesh: grp: 2 (over z_lo), seq: 8 (over y, core), head: 8 (over z_hi, x).
Axes of the slice: x: 4, y: 4, z: 4 (z_hi: 2, z_lo: 2; z = z_hi * 2 + z_lo), core: 2. Of those that a mesh axis runs over, the one named last changes fastest.
Arguments:
- encoder: bfloat16 [2, 16384, 1280], P('grp', ('seq', 'head')), may hold values from -6 to 6
- w_key: bfloat16 [1280, 1024], replicated, may hold values from -0.15625 to 0.15625
- w_value: bfloat16 [1280, 1024], replicated, may hold values from -0.15625 to 0.15625
- queries: bfloat16 [2, 4096, 1024], P('grp', 'seq', 'head'), may hold values from -60 to 60
- d_out: bfloat16 [2, 4096, 1024], P('grp', 'seq', 'head'), may hold values from -6 to 6
- n_frames: int32 [2], P('grp'), may hold values from 4096 to 16384
- t_len: int32 [2], P('grp'), may hold values from 1024 to 4096
Outputs:
- attended: bfloat16 [2, 4096, 1024], P('grp', 'seq', 'head')
- d_queries: bfloat16 [2, 4096, 1024], P('grp', 'seq', 'head')
- d_encoder: bfloat16 [2, 16384, 1280], P('grp', ('seq', 'head'))
The draws below stay inside these ranges and needn't reach their ends.
All inputs are finite; a program needn't handle non-finite values.
Results may differ from the reference program's by a relative error of at most 0.03.
The reference program's roundings to bfloat16 on the way (of `probs_low`, `grad_out` and `d_scores`) count: a program that leaves them out, or rounds other values in their place, can miss the bound.
Values may be sent and summed in bfloat16 or wider, within the bound.
No kernel may reach another device: no remote copies, remote signals or barrier semaphores. Data moves between devices by JAX's collectives and lax.ppermute only.
A program may use at most 128 MiB of HBM per device.

```python
import jax
import jax.numpy as jnp
from jax import lax

D = 1280
HEADS = 16
HDIM = 64
RECS = 2
FRAMES = 16384
LEN = 4096


def draw_queries(key, part):
    key = jax.random.fold_in(key, 11)
    shape = (RECS, LEN, HEADS * HDIM)
    base = jnp.clip(jax.random.normal(key, shape, jnp.float32), -6.0, 6.0)
    return base.astype(jnp.bfloat16)


def block_levels(rng, shape, split, least, top_value):
    def one(position, parts):
        draws = jax.random.uniform(jax.random.fold_in(jax.random.fold_in(rng, 6), position), (parts,), jnp.float32, least / len(split), top_value / len(split))
        return jnp.repeat(jnp.exp(draws), shape[position] // parts).reshape((-1,) + (1,) * (len(shape) - position - 1))

    factor_of = one(*split[0])
    for cut in split[1:]:
        factor_of = factor_of * one(*cut)
    return factor_of


def gaussian(stream_key, extent, spread, most, pieces=(), kind=jnp.bfloat16):
    loudness = block_levels(stream_key, extent, pieces, -0.22, 0.18) if pieces else 1.0
    entries = jax.random.normal(stream_key, extent, jnp.float32) * spread * loudness
    return jnp.minimum(jnp.maximum(entries, -most), most).astype(kind)


def setup_inputs(seed: int = 0) -> dict:
    seeds = jax.random.split(jax.random.key(seed), 8)
    return {
        "encoder": gaussian(seeds[0], (RECS, FRAMES, D), 1.0, 6.0, ((0, 2), (1, 64))),
        "w_key": gaussian(seeds[1], (D, HEADS * HDIM), D ** -0.5, 0.15625),
        "w_value": gaussian(seeds[2], (D, HEADS * HDIM), D ** -0.5, 0.15625),
        "queries": draw_queries(jax.random.fold_in(seeds[7], 71), 0),
        "d_out": gaussian(seeds[4], (RECS, LEN, HEADS * HDIM), 1.0, 6.0, ((0, 2), (1, 8), (2, 8))),
        "n_frames": jax.random.randint(seeds[5], (RECS,), FRAMES // 4, FRAMES + 1).astype(jnp.int32),
        "t_len": jax.random.randint(seeds[6], (RECS,), LEN // 4, LEN + 1).astype(jnp.int32),
    }


def head_pass(item, fvalid, tmask, scale):
    qh, kh, vh, gh = item
    s = jnp.dot(qh, kh.T, preferred_element_type=jnp.float32) * scale
    s = jnp.where(fvalid[None, :], s, -1e30)
    top = jnp.max(s, axis=1, keepdims=True)
    total = jnp.sum(jnp.where(fvalid[None, :], jnp.exp(s - top), 0.0), axis=1)
    lse = top[:, 0] + jnp.log(total)
    probs = jnp.where(fvalid[None, :], jnp.exp(s - lse[:, None]), 0.0)
    probs_low = probs.astype(jnp.bfloat16)
    out = jnp.dot(probs_low, vh, preferred_element_type=jnp.float32) * tmask[:, None].astype(jnp.float32)
    out_low = out.astype(jnp.bfloat16)
    delta = jnp.sum(gh.astype(jnp.float32) * out_low.astype(jnp.float32), axis=1)
    d_probs = jnp.dot(gh, vh.T, preferred_element_type=jnp.float32)
    d_scores = (probs * (d_probs - delta[:, None])).astype(jnp.bfloat16)
    dq = (jnp.dot(d_scores, kh, preferred_element_type=jnp.float32) * scale).astype(jnp.bfloat16)
    dk = (jnp.dot(d_scores.T, qh, preferred_element_type=jnp.float32) * scale).astype(jnp.bfloat16)
    dv = jnp.dot(probs_low.T, gh, preferred_element_type=jnp.float32).astype(jnp.bfloat16)
    return out_low, dq, dk, dv


def split_heads(x, rows):
    return x.reshape(rows, HEADS, HDIM).transpose(1, 0, 2)


def join_heads(x, rows):
    return x.transpose(1, 0, 2).reshape(rows, HEADS * HDIM)


def reference(encoder, w_key, w_value, queries, d_out, n_frames, t_len):
    scale = HDIM ** -0.5
    outs, dqs, dencs = [], [], []
    for r in range(RECS):
        keys = jnp.dot(encoder[r], w_key, preferred_element_type=jnp.float32).astype(jnp.bfloat16)
        values = jnp.dot(encoder[r], w_value, preferred_element_type=jnp.float32).astype(jnp.bfloat16)
        tmask = jnp.arange(LEN, dtype=jnp.int32) < t_len[r]
        fvalid = jnp.arange(FRAMES, dtype=jnp.int32) < n_frames[r]
        grad_out = jnp.where(tmask[:, None], d_out[r], jnp.zeros_like(d_out[r])).astype(jnp.bfloat16)
        items = (split_heads(queries[r], LEN), split_heads(keys, FRAMES), split_heads(values, FRAMES), split_heads(grad_out, LEN))
        out_low, dq, dk, dv = lax.map(lambda item: head_pass(item, fvalid, tmask, scale), items)
        d_keys = join_heads(dk, FRAMES)
        d_values = join_heads(dv, FRAMES)
        denc = jnp.dot(d_keys, w_key.T, preferred_element_type=jnp.float32) + jnp.dot(d_values, w_value.T, preferred_element_type=jnp.float32)
        outs.append(join_heads(out_low, LEN))
        dqs.append(join_heads(dq, LEN))
        dencs.append(denc.astype(jnp.bfloat16))
    return jnp.stack(outs), jnp.stack(dqs), jnp.stack(dencs)
```

```python
import functools

import jax
import jax.numpy as jnp
from jax import lax
from jax.experimental import pallas as pl
from jax.experimental.pallas import tpu as pltpu
from jax.sharding import PartitionSpec as P

HDIM = 64
LANES = 128
SCALE = HDIM ** (-0.5)
FRAME_TILE = 512
TOKEN_TILE = 512
SUB = 256
BF16 = jnp.bfloat16
F32 = jnp.float32
VMEM = pltpu.VMEM
MIB = 1 << 20


def dot(a, b):
    return jnp.dot(a, b, preferred_element_type=F32)


def dot_t(a, b):
    return lax.dot_general(a, b, (((1,), (1,)), ((), ())), preferred_element_type=F32)


def params(mib):
    return pltpu.CompilerParams(vmem_limit_bytes=mib * MIB)


def vmem_spec(count):
    return [pl.BlockSpec(memory_space=VMEM)] * count


def smem_spec():
    return pl.BlockSpec(memory_space=pltpu.SMEM)


def pack_kernel(lim_ref, q_ref, g_ref, out_ref):
    tok = q_ref.shape[0]
    row = lax.broadcasted_iota(jnp.int32, (tok, LANES), 0)
    q = (q_ref[...].astype(F32) * SCALE).astype(BF16)
    g = jnp.where(row < lim_ref[0], g_ref[...].astype(F32), 0.0).astype(BF16)
    out_ref[0] = jnp.concatenate([q[:, :HDIM], g[:, :HDIM]], axis=1)
    out_ref[1] = jnp.concatenate([q[:, HDIM:], g[:, HDIM:]], axis=1)


def project_kernel(x_ref, wk_ref, wv_ref, out_ref):
    parts, rows = out_ref.shape[1], out_ref.shape[3]
    w = jnp.concatenate([wk_ref[...], wv_ref[...]], axis=1)
    kv = dot(x_ref[...], w).astype(BF16)
    k, v = kv[:, :LANES], kv[:, LANES:]
    for g in range(2):
        cols = slice(g * HDIM, (g + 1) * HDIM)
        both = jnp.concatenate([k[:, cols], v[:, cols]], axis=1)
        out_ref[g, :, 0] = both.reshape(parts, rows, LANES)


def project(x, wk, wv, seq, head):
    frames, depth = x.shape
    rows = frames // seq
    return pl.pallas_call(
        project_kernel,
        grid=(head,),
        in_specs=[
            pl.BlockSpec((frames, depth), lambda i: (0, 0)),
            pl.BlockSpec((depth, LANES), lambda i: (0, i)),
            pl.BlockSpec((depth, LANES), lambda i: (0, i)),
        ],
        out_specs=pl.BlockSpec((2, seq, 1, rows, LANES), lambda i: (0, 0, i, 0, 0)),
        out_shape=jax.ShapeDtypeStruct((2, seq, head, rows, LANES), BF16),
        compiler_params=params(40),
        name="project",
    )(x, wk, wv)


def load_tokens(lim_ref, pieces, tok, store):
    for i, piece in enumerate(pieces):
        at = pl.multiple_of(lim_ref[4 + i] * tok, tok)
        for r in range(2):
            store(r, at, piece[r])


def load_frames(lim_ref, kv_ref, kvx_ref, kt_ref, which):
    frames = kv_ref.shape[1]
    for r in range(2):
        n = lim_ref[r]
        for at in range(0, frames, FRAME_TILE):
            size = min(FRAME_TILE, frames)
            rows = slice(at, at + size)
            blk = kv_ref[r, rows, :]
            row = lax.broadcasted_iota(jnp.int32, (size, LANES), 0) + at
            first = jnp.broadcast_to(kv_ref[r, 0:1, :].astype(F32), (size, LANES))
            kvx_ref[r, rows, :] = jnp.where(row < n, blk.astype(F32), first).astype(BF16)
            t = jnp.transpose(blk)[which * HDIM : (which + 1) * HDIM]
            col = lax.broadcasted_iota(jnp.int32, (HDIM, size), 1) + at
            kt_ref[r, 0:HDIM, rows] = jnp.where(col < n, t.astype(F32), 0.0).astype(BF16)
            if which == 1:
                sub = lax.broadcasted_iota(jnp.int32, (16, size), 0)
                col = lax.broadcasted_iota(jnp.int32, (16, size), 1) + at
                ones = jnp.where((sub == 0) & (col < n), 1.0, 0.0)
                kt_ref[r, HDIM : HDIM + 16, rows] = ones.astype(BF16)


def forward_kernel(pieces, lim_ref, kv_ref, *refs):
    piece_refs = refs[:pieces]
    o_ref, st_ref = refs[pieces : pieces + 2]
    kvx_ref, vt_ref, qt_ref, gt_ref, m_ref, acc_ref = refs[pieces + 2 :]
    tok = o_ref.shape[3]
    tile = min(TOKEN_TILE, tok)
    frames = kv_ref.shape[1]
    ftile = min(FRAME_TILE, frames)
    sub = min(SUB, tile)

    def store(r, at, blk):
        t = jnp.transpose(blk)
        zero = jnp.zeros((HDIM, tok), BF16)
        qt_ref[r, :, pl.ds(at, tok)] = jnp.concatenate([t[:HDIM], zero], axis=0)
        gt_ref[r, :, pl.ds(at, tok)] = t[HDIM:]

    load_tokens(lim_ref, piece_refs, tok, store)
    load_frames(lim_ref, kv_ref, kvx_ref, vt_ref, 1)
    o_ref[...] = jnp.zeros_like(o_ref)
    st_ref[...] = jnp.zeros_like(st_ref)

    for r in range(2):
        limit = lim_ref[2 + r]
        n_f = pl.cdiv(lim_ref[r], ftile)

        def tokens(tt, _, r=r, limit=limit, n_f=n_f):
            at = pl.multiple_of(tt * tile, tile)
            m_ref[...] = jnp.full(m_ref.shape, -3e38, F32)
            acc_ref[...] = jnp.zeros_like(acc_ref)

            def step(ff, _):
                fat = pl.multiple_of(ff * ftile, ftile)
                kv = kvx_ref[r, pl.ds(fat, ftile), :]
                vt = vt_ref[r, :, pl.ds(fat, ftile)]
                for c in range(0, tile, sub):
                    cols = slice(c, c + sub)
                    s = dot(kv, qt_ref[r, :, pl.ds(at + c, sub)])
                    old = m_ref[0:1, cols]
                    new = jnp.maximum(old, jnp.max(s, axis=0, keepdims=True))
                    p = jnp.exp(s - new).astype(BF16)
                    acc_ref[:, cols] = acc_ref[:, cols] * jnp.exp(old - new) + dot(vt, p)
                    m_ref[0:1, cols] = new
                return 0

            lax.fori_loop(0, n_f, step, 0)
            total = acc_ref[HDIM : HDIM + 1, :]
            o = acc_ref[0:HDIM, :] * (1.0 / total)
            g = gt_ref[r, :, pl.ds(at, tile)].astype(F32)
            col = lax.broadcasted_iota(jnp.int32, (HDIM, tile), 1) + at
            where = (r, at // tok, slice(None), pl.ds(pl.multiple_of(at % tok, tile), tile))
            o_ref[where] = jnp.where(col < limit, o, 0.0)
            st_ref[r : r + 1, pl.ds(at, tile)] = m_ref[0:1, :] + jnp.log(total)
            st_ref[2 + r : 3 + r, pl.ds(at, tile)] = jnp.sum(o * g, axis=0, keepdims=True)
            return 0

        lax.fori_loop(0, pl.cdiv(limit, tile), tokens, 0)


def forward(lim, kv, pieces):
    tok = pieces[0].shape[1]
    count = len(pieces)
    length = tok * count
    frames = kv.shape[1]
    return pl.pallas_call(
        functools.partial(forward_kernel, count),
        in_specs=[smem_spec()] + vmem_spec(1 + count),
        out_specs=vmem_spec(2),
        out_shape=[
            jax.ShapeDtypeStruct((2, count, HDIM, tok), F32),
            jax.ShapeDtypeStruct((4, length), F32),
        ],
        scratch_shapes=[
            VMEM((2, frames, LANES), BF16),
            VMEM((2, HDIM + 16, frames), BF16),
            VMEM((2, LANES, length), BF16),
            VMEM((2, HDIM, length), BF16),
            VMEM((8, min(TOKEN_TILE, tok)), F32),
            VMEM((HDIM + 16, min(TOKEN_TILE, tok)), F32),
        ],
        compiler_params=params(48),
        name="forward",
    )(lim, kv, *pieces)


def combine_kernel(count, o_ref, *refs):
    st_refs = refs[:count]
    out_ref, stat_ref = refs[count:]
    tok = o_ref.shape[3]
    for r in range(2):
        tops = [st[r : r + 1, :] for st in st_refs]
        top = functools.reduce(jnp.maximum, tops)
        weights = [jnp.exp(t - top) for t in tops]
        total = functools.reduce(jnp.add, weights)
        inverse = 1.0 / total
        delta = functools.reduce(jnp.add, [w * st[2 + r : 3 + r, :] for w, st in zip(weights, st_refs)])
        stat_ref[r : r + 1, :] = top + jnp.log(total)
        stat_ref[2 + r : 3 + r, :] = delta * inverse
        mine = weights[0] * inverse
        for b in range(o_ref.shape[1]):
            out_ref[r, b] = (o_ref[r, b] * mine[:, b * tok : (b + 1) * tok]).astype(BF16)


def combine(o, stats):
    count = len(stats)
    return pl.pallas_call(
        functools.partial(combine_kernel, count),
        in_specs=vmem_spec(1 + count),
        out_specs=vmem_spec(2),
        out_shape=[
            jax.ShapeDtypeStruct(o.shape, BF16),
            jax.ShapeDtypeStruct(stats[0].shape, F32),
        ],
        compiler_params=params(40),
        name="combine",
    )(o, *stats)


def backward_kernel(pieces, lim_ref, kv_ref, stat_ref, *refs):
    piece_refs = refs[:pieces]
    dkv_ref, dq_ref = refs[pieces : pieces + 2]
    kvx_ref, kt_ref, qt_ref, gt_ref, q_ref, g_ref, dq_acc, dkv_acc = refs[pieces + 2 :]
    tok = dq_ref.shape[3]
    tile = min(TOKEN_TILE, tok)
    frames = kv_ref.shape[1]
    ftile = min(FRAME_TILE, frames)
    sub = min(SUB, tile)

    def store(r, at, blk):
        t = jnp.transpose(blk)
        zero = jnp.zeros((HDIM, tok), BF16)
        qt_ref[r, :, pl.ds(at, tok)] = jnp.concatenate([t[:HDIM], zero], axis=0)
        gt_ref[r, :, pl.ds(at, tok)] = jnp.concatenate([zero, t[HDIM:]], axis=0)
        lane = lax.broadcasted_iota(jnp.int32, (tok, LANES), 1)
        wide = blk.astype(F32)
        q_ref[r, pl.ds(at, tok), :] = jnp.where(lane < HDIM, wide, 0.0).astype(BF16)
        g_ref[r, pl.ds(at, tok), :] = jnp.where(lane < HDIM, 0.0, wide).astype(BF16)

    load_tokens(lim_ref, piece_refs, tok, store)
    load_frames(lim_ref, kv_ref, kvx_ref, kt_ref, 0)
    dkv_ref[...] = jnp.zeros_like(dkv_ref)
    dq_acc[...] = jnp.zeros_like(dq_acc)

    for r in range(2):
        n = lim_ref[r]
        n_t = pl.cdiv(lim_ref[2 + r], tile)

        def blocks(ff, _, r=r, n=n, n_t=n_t):
            fat = pl.multiple_of(ff * ftile, ftile)
            kv = kvx_ref[r, pl.ds(fat, ftile), :]
            kt = kt_ref[r, :, pl.ds(fat, ftile)]
            dkv_acc[...] = jnp.zeros_like(dkv_acc)

            def step(tt, _):
                at = pl.multiple_of(tt * tile, tile)
                low, dlow = [], []
                for c in range(0, tile, sub):
                    cols = pl.ds(at + c, sub)
                    s = dot(kv, qt_ref[r, :, cols])
                    dp = dot(kv, gt_ref[r, :, cols])
                    p = jnp.exp(s - stat_ref[r : r + 1, cols])
                    ds = (p * (dp - stat_ref[2 + r : 3 + r, cols])).astype(BF16)
                    dq_acc[r, :, cols] += dot(kt, ds)
                    low.append(p.astype(BF16))
                    dlow.append(ds)
                left = jnp.concatenate(dlow + low, axis=1)
                rows = pl.ds(at, tile)
                right = jnp.concatenate([q_ref[r, rows, :], g_ref[r, rows, :]], axis=0)
                dkv_acc[...] += dot(left, right)
                return 0

            lax.fori_loop(0, n_t, step, 0)
            row = lax.broadcasted_iota(jnp.int32, (ftile, LANES), 0) + fat
            dkv_ref[r, pl.ds(fat, ftile), :] = jnp.where(row < n, dkv_acc[...], 0.0).astype(BF16)
            return 0

        lax.fori_loop(0, pl.cdiv(n, ftile), blocks, 0)
        for b in range(dq_ref.shape[1]):
            dq_ref[r, b] = (dq_acc[r, :, b * tok : (b + 1) * tok] * SCALE).astype(BF16)


def backward(lim, kv, stat, pieces):
    tok = pieces[0].shape[1]
    count = len(pieces)
    length = tok * count
    frames = kv.shape[1]
    return pl.pallas_call(
        functools.partial(backward_kernel, count),
        in_specs=[smem_spec()] + vmem_spec(2 + count),
        out_specs=vmem_spec(2),
        out_shape=[
            jax.ShapeDtypeStruct(kv.shape, BF16),
            jax.ShapeDtypeStruct((2, count, HDIM, tok), BF16),
        ],
        scratch_shapes=[
            VMEM((2, frames, LANES), BF16),
            VMEM((2, HDIM, frames), BF16),
            VMEM((2, LANES, length), BF16),
            VMEM((2, LANES, length), BF16),
            VMEM((2, length, LANES), BF16),
            VMEM((2, length, LANES), BF16),
            VMEM((2, HDIM, length), F32),
            VMEM((min(FRAME_TILE, frames), LANES), F32),
        ],
        compiler_params=params(48),
        name="backward",
    )(lim, kv, stat, *pieces)


def gather_kernel(x_ref, out_ref):
    halves = []
    for g in range(2):
        total = x_ref[g, 0].astype(F32)
        for s in range(1, x_ref.shape[1]):
            total = total + x_ref[g, s].astype(F32)
        halves.append(total)
    out_ref[...] = jnp.transpose(jnp.concatenate(halves, axis=0)).astype(BF16)


def gather(x):
    tok = x.shape[3]
    return pl.pallas_call(
        gather_kernel,
        in_specs=vmem_spec(1),
        out_specs=pl.BlockSpec(memory_space=VMEM),
        out_shape=jax.ShapeDtypeStruct((tok, LANES), BF16),
        compiler_params=params(40),
        name="gather",
    )(x)


def encoder_kernel(d_ref, wk_ref, wv_ref, out_ref):
    heads = d_ref.shape[2]
    rows = d_ref.shape[1] * d_ref.shape[3]
    acc = None
    for h in range(heads):
        a = d_ref[0, :, h].reshape(rows, LANES)
        b = d_ref[1, :, h].reshape(rows, LANES)
        dk = jnp.concatenate([a[:, :HDIM], b[:, :HDIM]], axis=1)
        dv = jnp.concatenate([a[:, HDIM:], b[:, HDIM:]], axis=1)
        cols = slice(h * LANES, (h + 1) * LANES)
        left = jnp.concatenate([dk, dv], axis=1)
        right = jnp.concatenate([wk_ref[:, cols], wv_ref[:, cols]], axis=1)
        part = dot_t(left, right)
        acc = part if acc is None else acc + part
    out_ref[...] = acc.astype(BF16)


def encoder_grad(d, wk, wv):
    rows = d.shape[1] * d.shape[3]
    return pl.pallas_call(
        encoder_kernel,
        in_specs=vmem_spec(3),
        out_specs=pl.BlockSpec(memory_space=VMEM),
        out_shape=jax.ShapeDtypeStruct((rows, wk.shape[0]), BF16),
        compiler_params=params(40),
        name="encoder_grad",
    )(d, wk, wv)


def on_device(grp, seq, head, encoder, w_key, w_value, queries, d_out, n_frames, t_len):
    every = ("grp", "seq", "head")
    me_g, me_s = lax.axis_index("grp"), lax.axis_index("seq")
    other = [(0, 1), (1, 0)]

    def by_grp(own, received):
        return jnp.where(me_g == 0, jnp.stack([own, received]), jnp.stack([received, own]))

    def around(x, k):
        return lax.ppermute(x, "seq", [(i, i ^ k) for i in range(seq)])

    def over_seq(x):
        parts = [x] + [around(x, k) for k in range(2, seq, 2)]
        return parts + [around(p, 1) for p in parts]

    tok = queries.shape[1]
    frames = encoder.shape[1]
    rows = frames // seq
    bounds = jnp.concatenate([n_frames, t_len])
    bounds2 = by_grp(bounds, lax.ppermute(bounds, "grp", other))
    whole = (bounds2[:, 0] // frames) * rows
    n_here = whole + jnp.clip(bounds2[:, 0] % frames - rows * me_s, 0, rows)
    blocks = jnp.array([k for k in range(0, seq, 2)] + [k + 1 for k in range(0, seq, 2)], jnp.int32)
    lim = jnp.concatenate([n_here, bounds2[:, 1], blocks ^ me_s]).astype(jnp.int32)

    packed = pl.pallas_call(
        pack_kernel,
        in_specs=[smem_spec()] + vmem_spec(2),
        out_specs=pl.BlockSpec(memory_space=VMEM),
        out_shape=jax.ShapeDtypeStruct((2, tok, LANES), BF16),
        compiler_params=params(40),
        name="pack",
    )(t_len - me_s * tok, queries[0], d_out[0])
    sent = lax.ppermute(lax.dynamic_index_in_dim(packed, 1 - me_g, 0, keepdims=False), "grp", other)
    kept = lax.dynamic_index_in_dim(packed, me_g, 0, keepdims=False)
    pieces = over_seq(by_grp(kept, sent))

    kv = project(encoder[0], w_key, w_value, seq, head)
    kv = lax.all_to_all(kv.reshape(grp * seq * head, rows, LANES), every, 0, 0, tiled=True)
    kv = kv.reshape(2, seq * head * rows, LANES)
    o_part, stats = forward(lim, kv, pieces)
    o_part, stat = combine(o_part, over_seq(stats))
    o_all = lax.all_to_all(o_part.reshape(grp * seq, HDIM, tok), ("grp", "seq"), 0, 0, tiled=True)
    attended = gather(o_all.reshape(2, seq, HDIM, tok))
    d_kv, dq_part = backward(lim, kv, stat, pieces)
    d_kv = lax.all_to_all(d_kv.reshape(grp * seq * head, rows, LANES), every, 0, 0, tiled=True)
    dq_all = lax.all_to_all(dq_part.reshape(grp * seq, HDIM, tok), ("grp", "seq"), 0, 0, tiled=True)
    d_query = gather(dq_all.reshape(2, seq, HDIM, tok))
    d_states = encoder_grad(d_kv.reshape(2, seq, head, rows, LANES), w_key, w_value)
    return attended[None], d_query[None], d_states[None]


def solution(mesh):
    sizes = mesh.shape
    return jax.shard_map(
        functools.partial(on_device, sizes["grp"], sizes["seq"], sizes["head"]),
        mesh=mesh,
        in_specs=(
            P("grp", ("seq", "head"), None),
            P(),
            P(),
            P("grp", "seq", "head"),
            P("grp", "seq", "head"),
            P("grp"),
            P("grp"),
        ),
        out_specs=(
            P("grp", "seq", "head"),
            P("grp", "seq", "head"),
            P("grp", ("seq", "head"), None),
        ),
        check_vma=False,
    )
```

```python
import functools

import jax
import jax.numpy as jnp
from jax import lax
from jax.experimental import pallas as pl
from jax.experimental.pallas import tpu as pltpu
from jax.sharding import PartitionSpec as P

HDIM = 64
LANES = 128
SCALE = HDIM ** (-0.5)
FRAME_TILE = 512
TOKEN_TILE = 512
SUB = 256
BF16 = jnp.bfloat16
F32 = jnp.float32
VMEM = pltpu.VMEM
MIB = 1 << 20


def dot(a, b):
    return jnp.dot(a, b, preferred_element_type=F32)


def dot_t(a, b):
    return lax.dot_general(a, b, (((1,), (1,)), ((), ())), preferred_element_type=F32)


def params(mib):
    return pltpu.CompilerParams(vmem_limit_bytes=mib * MIB)


def vmem_spec(count):
    return [pl.BlockSpec(memory_space=VMEM)] * count


def smem_spec():
    return pl.BlockSpec(memory_space=pltpu.SMEM)


def pack_kernel(lim_ref, q_ref, g_ref, own_ref, pair_ref):
    tok = q_ref.shape[0]
    row = lax.broadcasted_iota(jnp.int32, (tok, LANES), 0)
    q = q_ref[...].astype(F32) * SCALE
    g = jnp.where(row < lim_ref[0], g_ref[...].astype(F32), 0.0)
    low = jnp.concatenate([q[:, :HDIM], g[:, :HDIM]], axis=1)
    high = jnp.concatenate([q[:, HDIM:], g[:, HDIM:]], axis=1)
    first = lim_ref[1] == 0
    own_ref[...] = jnp.where(first, low, high).astype(BF16)
    pair_ref[...] = jnp.where(first, high, low).astype(BF16)


def pack(lim, q, g):
    shape = jax.ShapeDtypeStruct(q.shape, BF16)
    return pl.pallas_call(
        pack_kernel,
        in_specs=[smem_spec()] + vmem_spec(2),
        out_specs=vmem_spec(2),
        out_shape=[shape, shape],
        compiler_params=params(40),
        name="pack",
    )(lim, q, g)


def project_kernel(x_ref, wk_ref, wv_ref, out_ref):
    parts, rows = out_ref.shape[1], out_ref.shape[3]
    w = jnp.concatenate([wk_ref[...], wv_ref[...]], axis=1)
    kv = dot(x_ref[...], w).astype(BF16)
    k, v = kv[:, :LANES], kv[:, LANES:]
    for g in range(2):
        cols = slice(g * HDIM, (g + 1) * HDIM)
        both = jnp.concatenate([k[:, cols], v[:, cols]], axis=1)
        out_ref[g, :, 0] = both.reshape(parts, rows, LANES)


def project(x, wk, wv, seq, head):
    frames, depth = x.shape
    rows = frames // seq
    return pl.pallas_call(
        project_kernel,
        grid=(head,),
        in_specs=[
            pl.BlockSpec((frames, depth), lambda i: (0, 0)),
            pl.BlockSpec((depth, LANES), lambda i: (0, i)),
            pl.BlockSpec((depth, LANES), lambda i: (0, i)),
        ],
        out_specs=pl.BlockSpec((2, seq, 1, rows, LANES), lambda i: (0, 0, i, 0, 0)),
        out_shape=jax.ShapeDtypeStruct((2, seq, head, rows, LANES), BF16),
        compiler_params=params(40),
        name="project",
    )(x, wk, wv)


def load_tokens(lim_ref, pieces, store):
    tok = pieces[0].shape[0]
    for i, piece in enumerate(pieces):
        store(pl.multiple_of(lim_ref[5 + i] * tok, tok), piece[...])


def load_frames(n, kv_ref, r, kvx_ref, kt_ref, which):
    frames = kv_ref.shape[1]
    size = min(FRAME_TILE, frames)
    first = kv_ref[r, 0:1, :].astype(F32)
    for at in range(0, frames, size):
        rows = slice(at, at + size)
        blk = kv_ref[r, rows, :]
        row = lax.broadcasted_iota(jnp.int32, (size, LANES), 0) + at
        kvx_ref[rows, :] = jnp.where(row < n, blk.astype(F32), first).astype(BF16)
        t = jnp.transpose(blk)[which * HDIM : (which + 1) * HDIM]
        col = lax.broadcasted_iota(jnp.int32, (HDIM, size), 1) + at
        kt_ref[0:HDIM, rows] = jnp.where(col < n, t.astype(F32), 0.0).astype(BF16)
        if which == 1:
            sub = lax.broadcasted_iota(jnp.int32, (16, size), 0)
            col = lax.broadcasted_iota(jnp.int32, (16, size), 1) + at
            ones = jnp.where((sub == 0) & (col < n), 1.0, 0.0)
            kt_ref[HDIM : HDIM + 16, rows] = ones.astype(BF16)


def put_block(lim_ref, block, cols, value, keep_ref, send_ref):
    mine = lax.rem(block, 2) == lim_ref[3]
    chip = block // 2

    @pl.when(mine)
    def _():
        keep_ref[chip, :, cols] = value

    @pl.when(jnp.logical_not(mine))
    def _():
        send_ref[chip, :, cols] = value.astype(BF16)


def forward_kernel(pieces, lim_ref, kv_ref, *refs):
    piece_refs = refs[:pieces]
    keep_ref, send_ref, st_ref = refs[pieces : pieces + 3]
    kvx_ref, vt_ref, qt_ref, gt_ref, m_ref, acc_ref = refs[pieces + 3 :]
    tok = keep_ref.shape[2]
    tile = min(TOKEN_TILE, tok)
    frames = kv_ref.shape[1]
    ftile = min(FRAME_TILE, frames)
    sub = min(SUB, tile)
    n, limit = lim_ref[0], lim_ref[1]

    def store(at, blk):
        t = jnp.transpose(blk)
        qt_ref[:, pl.ds(at, tok)] = jnp.concatenate([t[:HDIM], jnp.zeros((HDIM, tok), BF16)], axis=0)
        gt_ref[:, pl.ds(at, tok)] = t[HDIM:]

    load_tokens(lim_ref, piece_refs, store)
    load_frames(n, kv_ref, lim_ref[2], kvx_ref, vt_ref, 1)
    keep_ref[...] = jnp.zeros_like(keep_ref)
    send_ref[...] = jnp.zeros_like(send_ref)
    st_ref[...] = jnp.zeros_like(st_ref)

    def tokens(tt, _):
        at = pl.multiple_of(tt * tile, tile)
        m_ref[...] = jnp.full(m_ref.shape, -3e38, F32)
        acc_ref[...] = jnp.zeros_like(acc_ref)

        def step(ff, _):
            fat = pl.multiple_of(ff * ftile, ftile)
            kv = kvx_ref[pl.ds(fat, ftile), :]
            vt = vt_ref[:, pl.ds(fat, ftile)]
            for c in range(0, tile, sub):
                cols = slice(c, c + sub)
                s = dot(kv, qt_ref[:, pl.ds(at + c, sub)])
                old = m_ref[0:1, cols]
                new = jnp.maximum(old, jnp.max(s, axis=0, keepdims=True))
                p = jnp.exp(s - new).astype(BF16)
                acc_ref[:, cols] = acc_ref[:, cols] * jnp.exp(old - new) + dot(vt, p)
                m_ref[0:1, cols] = new
            return 0

        lax.fori_loop(0, pl.cdiv(n, ftile), step, 0)
        total = acc_ref[HDIM : HDIM + 1, :]
        o = acc_ref[0:HDIM, :] * (1.0 / total)
        g = gt_ref[:, pl.ds(at, tile)].astype(F32)
        col = lax.broadcasted_iota(jnp.int32, (HDIM, tile), 1) + at
        cols = pl.ds(pl.multiple_of(lax.rem(at, tok), tile), tile)
        put_block(lim_ref, at // tok, cols, jnp.where(col < limit, o, 0.0), keep_ref, send_ref)
        st_ref[0:1, pl.ds(at, tile)] = m_ref[0:1, :] + jnp.log(total)
        st_ref[1:2, pl.ds(at, tile)] = jnp.sum(o * g, axis=0, keepdims=True)
        return 0

    lax.fori_loop(0, pl.cdiv(limit, tile), tokens, 0)


def forward(lim, kv, pieces):
    tok = pieces[0].shape[0]
    count = len(pieces)
    length = tok * count
    frames = kv.shape[1]
    return pl.pallas_call(
        functools.partial(forward_kernel, count),
        in_specs=[smem_spec()] + vmem_spec(1 + count),
        out_specs=vmem_spec(3),
        out_shape=[
            jax.ShapeDtypeStruct((count // 2, HDIM, tok), F32),
            jax.ShapeDtypeStruct((count // 2, HDIM, tok), BF16),
            jax.ShapeDtypeStruct((2, length), F32),
        ],
        scratch_shapes=[
            VMEM((frames, LANES), BF16),
            VMEM((HDIM + 16, frames), BF16),
            VMEM((LANES, length), BF16),
            VMEM((HDIM, length), BF16),
            VMEM((8, min(TOKEN_TILE, tok)), F32),
            VMEM((HDIM + 16, min(TOKEN_TILE, tok)), F32),
        ],
        compiler_params=params(48),
        name="forward",
    )(lim, kv, *pieces)


def stats_kernel(count, *refs):
    st_refs = refs[:count]
    stat_ref, mine_ref, pair_ref = refs[count:]
    tops = [st[0:1, :] for st in st_refs]
    top = functools.reduce(jnp.maximum, tops)
    weights = [jnp.exp(t - top) for t in tops]
    total = functools.reduce(jnp.add, weights)
    inverse = 1.0 / total
    delta = functools.reduce(jnp.add, [w * st[1:2, :] for w, st in zip(weights, st_refs)])
    stat_ref[0:1, :] = top + jnp.log(total)
    stat_ref[1:2, :] = delta * inverse
    mine_ref[...] = weights[0] * inverse
    pair_ref[...] = weights[count // 2] * inverse


def combine_stats(stats):
    count = len(stats)
    length = stats[0].shape[1]
    row = jax.ShapeDtypeStruct((1, length), F32)
    return pl.pallas_call(
        functools.partial(stats_kernel, count),
        in_specs=vmem_spec(count),
        out_specs=vmem_spec(3),
        out_shape=[jax.ShapeDtypeStruct((2, length), F32), row, row],
        compiler_params=params(40),
        name="combine_stats",
    )(*stats)


def pair_kernel(weighted, lim_ref, *refs):
    if weighted:
        mine_ref, other_ref, keep_ref, got_ref, *outs = refs
    else:
        keep_ref, got_ref, *outs = refs
    tok = keep_ref.shape[2]
    for i, out in enumerate(outs):
        chip = lim_ref[4] ^ i
        a, b = keep_ref[chip], got_ref[chip].astype(F32)
        if weighted:
            cols = pl.ds(pl.multiple_of((chip * 2 + lim_ref[3]) * tok, tok), tok)
            a, b = a * mine_ref[0:1, cols], b * other_ref[0:1, cols]
        out[...] = (a + b).astype(BF16)


def add_pair(lim, keep, got, weights=()):
    count, rows, tok = keep.shape
    shape = jax.ShapeDtypeStruct((rows, tok), BF16)
    return pl.pallas_call(
        functools.partial(pair_kernel, bool(weights)),
        in_specs=[smem_spec()] + vmem_spec(2 + len(weights)),
        out_specs=vmem_spec(count),
        out_shape=[shape] * count,
        compiler_params=params(40),
        name="add_pair",
    )(lim, *weights, keep, got)


def backward_kernel(pieces, second, lim_ref, kv_ref, stat_ref, *refs):
    piece_refs = refs[:pieces]
    refs = refs[pieces:]
    if second:
        before_ref, refs = refs[0], refs[1:]
    dkv_ref, keep_ref, send_ref = refs[:3]
    kvx_ref, kt_ref, qt_ref, gt_ref, q_ref, g_ref, dq_acc, dkv_acc = refs[3:]
    tok = keep_ref.shape[2]
    tile = min(TOKEN_TILE, tok)
    frames = kv_ref.shape[1]
    ftile = min(FRAME_TILE, frames)
    sub = min(SUB, tile)
    n, limit, r = lim_ref[0], lim_ref[1], lim_ref[2]

    def store(at, blk):
        t = jnp.transpose(blk)
        zero = jnp.zeros((HDIM, tok), BF16)
        qt_ref[:, pl.ds(at, tok)] = jnp.concatenate([t[:HDIM], zero], axis=0)
        gt_ref[:, pl.ds(at, tok)] = jnp.concatenate([zero, t[HDIM:]], axis=0)
        lane = lax.broadcasted_iota(jnp.int32, (tok, LANES), 1)
        wide = blk.astype(F32)
        q_ref[pl.ds(at, tok), :] = jnp.where(lane < HDIM, wide, 0.0).astype(BF16)
        g_ref[pl.ds(at, tok), :] = jnp.where(lane < HDIM, 0.0, wide).astype(BF16)

    load_tokens(lim_ref, piece_refs, store)
    load_frames(n, kv_ref, r, kvx_ref, kt_ref, 0)
    if second:
        dkv_ref[1 - r] = before_ref[...]
        out = (r,)
    else:
        out = ()
    dkv_ref[out + (slice(None), slice(None))] = jnp.zeros((frames, LANES), BF16)
    dq_acc[...] = jnp.zeros_like(dq_acc)
    n_t = pl.cdiv(limit, tile)

    def blocks(ff, _):
        fat = pl.multiple_of(ff * ftile, ftile)
        kv = kvx_ref[pl.ds(fat, ftile), :]
        kt = kt_ref[:, pl.ds(fat, ftile)]
        dkv_acc[...] = jnp.zeros_like(dkv_acc)

        def step(tt, _):
            at = pl.multiple_of(tt * tile, tile)
            low, dlow = [], []
            for c in range(0, tile, sub):
                cols = pl.ds(at + c, sub)
                s = dot(kv, qt_ref[:, cols])
                dp = dot(kv, gt_ref[:, cols])
                p = jnp.exp(s - stat_ref[0:1, cols])
                ds = (p * (dp - stat_ref[1:2, cols])).astype(BF16)
                dq_acc[:, cols] += dot(kt, ds)
                low.append(p.astype(BF16))
                dlow.append(ds)
            left = jnp.concatenate(dlow + low, axis=1)
            rows = pl.ds(at, tile)
            right = jnp.concatenate([q_ref[rows, :], g_ref[rows, :]], axis=0)
            dkv_acc[...] += dot(left, right)
            return 0

        lax.fori_loop(0, n_t, step, 0)
        row = lax.broadcasted_iota(jnp.int32, (ftile, LANES), 0) + fat
        dkv_ref[out + (pl.ds(fat, ftile), slice(None))] = jnp.where(row < n, dkv_acc[...], 0.0).astype(BF16)
        return 0

    lax.fori_loop(0, pl.cdiv(n, ftile), blocks, 0)
    for b in range(pieces):
        put_block(lim_ref, jnp.int32(b), slice(None), dq_acc[:, b * tok : (b + 1) * tok] * SCALE, keep_ref, send_ref)


def backward(lim, kv, stat, pieces, before=None):
    tok = pieces[0].shape[0]
    count = len(pieces)
    length = tok * count
    frames = kv.shape[1]
    extra = [] if before is None else [before]
    return pl.pallas_call(
        functools.partial(backward_kernel, count, before is not None),
        in_specs=[smem_spec()] + vmem_spec(2 + count + len(extra)),
        out_specs=vmem_spec(3),
        out_shape=[
            jax.ShapeDtypeStruct(kv.shape[1:] if before is None else kv.shape, BF16),
            jax.ShapeDtypeStruct((count // 2, HDIM, tok), F32),
            jax.ShapeDtypeStruct((count // 2, HDIM, tok), BF16),
        ],
        scratch_shapes=[
            VMEM((frames, LANES), BF16),
            VMEM((HDIM, frames), BF16),
            VMEM((LANES, length), BF16),
            VMEM((LANES, length), BF16),
            VMEM((length, LANES), BF16),
            VMEM((length, LANES), BF16),
            VMEM((HDIM, length), F32),
            VMEM((min(FRAME_TILE, frames), LANES), F32),
        ],
        compiler_params=params(48),
        name="backward",
    )(lim, kv, stat, *pieces, *extra)


def gather_kernel(count, me_ref, *refs):
    mine, other, out_ref = refs[:count], refs[count : 2 * count], refs[2 * count]
    a = functools.reduce(jnp.add, [x[...].astype(F32) for x in mine])
    b = functools.reduce(jnp.add, [x[...].astype(F32) for x in other])
    first = me_ref[0] == 0
    both = jnp.concatenate([jnp.where(first, a, b), jnp.where(first, b, a)], axis=0)
    out_ref[...] = jnp.transpose(both).astype(BF16)


def gather(me, mine, other):
    tok = mine[0].shape[1]
    return pl.pallas_call(
        functools.partial(gather_kernel, len(mine)),
        in_specs=[smem_spec()] + vmem_spec(2 * len(mine)),
        out_specs=pl.BlockSpec(memory_space=VMEM),
        out_shape=jax.ShapeDtypeStruct((tok, LANES), BF16),
        compiler_params=params(40),
        name="gather",
    )(me, *mine, *other)


def encoder_kernel(d_ref, wk_ref, wv_ref, out_ref):
    heads = d_ref.shape[2]
    rows = d_ref.shape[1] * d_ref.shape[3]
    acc = None
    for h in range(heads):
        a = d_ref[0, :, h].reshape(rows, LANES)
        b = d_ref[1, :, h].reshape(rows, LANES)
        dk = jnp.concatenate([a[:, :HDIM], b[:, :HDIM]], axis=1)
        dv = jnp.concatenate([a[:, HDIM:], b[:, HDIM:]], axis=1)
        cols = slice(h * LANES, (h + 1) * LANES)
        left = jnp.concatenate([dk, dv], axis=1)
        right = jnp.concatenate([wk_ref[:, cols], wv_ref[:, cols]], axis=1)
        part = dot_t(left, right)
        acc = part if acc is None else acc + part
    out_ref[...] = acc.astype(BF16)


def encoder_grad(d, wk, wv):
    rows = d.shape[1] * d.shape[3]
    return pl.pallas_call(
        encoder_kernel,
        in_specs=vmem_spec(3),
        out_specs=pl.BlockSpec(memory_space=VMEM),
        out_shape=jax.ShapeDtypeStruct((rows, wk.shape[0]), BF16),
        compiler_params=params(40),
        name="encoder_grad",
    )(d, wk, wv)


def on_device(grp, seq, head, encoder, w_key, w_value, queries, d_out, n_frames, t_len):
    every = ("grp", "seq", "head")
    me_g, me_s = lax.axis_index("grp"), lax.axis_index("seq")
    chips = seq // 2

    def away(x, i, cross=False):
        if cross:
            pairs = [(g * seq + s, (1 - g) * seq + (s ^ (2 * i))) for g in range(grp) for s in range(seq)]
            return lax.ppermute(x, ("grp", "seq"), pairs)
        return x if i == 0 else lax.ppermute(x, "seq", [(s, s ^ (2 * i)) for s in range(seq)])

    def to_pair(x):
        return lax.ppermute(x, "seq", [(s, s ^ 1) for s in range(seq)])

    def over_seq(x, cross=False):
        parts = [away(x, i, cross) for i in range(chips)]
        return parts + [to_pair(p) for p in parts]

    tok = queries.shape[1]
    frames = encoder.shape[1]
    rows = frames // seq
    bounds = jnp.concatenate([n_frames, t_len])
    bounds = [bounds, lax.ppermute(bounds, "grp", [(0, 1), (1, 0)])]
    blocks = jnp.array([2 * i for i in range(chips)] + [2 * i + 1 for i in range(chips)], jnp.int32) ^ me_s

    def limits(rd):
        n, t = bounds[rd][0], bounds[rd][1]
        here = (n // frames) * rows + jnp.clip(n % frames - rows * me_s, 0, rows)
        head_part = jnp.stack([here, t, me_g ^ rd, me_s % 2, me_s // 2])
        return jnp.concatenate([head_part, blocks]).astype(jnp.int32)

    lims = [limits(0), limits(1)]
    own, pair = pack(jnp.stack([t_len[0] - me_s * tok, me_g]), queries[0], d_out[0])
    pieces = [over_seq(own), over_seq(pair, True)]

    states, _, _ = lax.optimization_barrier((encoder[0], own, pair))
    kv = project(states, w_key, w_value, seq, head)
    kv = lax.all_to_all(kv.reshape(grp * seq * head, rows, LANES), every, 0, 0, tiled=True)
    kv = kv.reshape(2, seq * head * rows, LANES)

    stat, o_parts, dq_parts = [], [], []
    for rd in range(2):
        keep, send, local = forward(lims[rd], kv, pieces[rd])
        whole, mine, other = combine_stats(over_seq(local))
        stat.append(whole)
        o_parts.append(add_pair(lims[rd], keep, to_pair(send), (mine, other)))
    d_kv = None
    for rd in range(2):
        d_kv, keep, send = backward(lims[rd], kv, stat[rd], pieces[rd], d_kv)
        dq_parts.append((keep, send))
    d_kv = lax.all_to_all(d_kv.reshape(grp * seq * head, rows, LANES), every, 0, 0, tiled=True)
    dq_parts = [add_pair(lims[rd], keep, to_pair(send)) for rd, (keep, send) in enumerate(dq_parts)]

    def finish(parts):
        got = [[away(parts[rd][i], i, rd == 1) for i in range(chips)] for rd in range(2)]
        return gather(me_g.reshape(1).astype(jnp.int32), *got)

    attended = finish(o_parts)
    d_query = finish(dq_parts)
    d_states = encoder_grad(d_kv.reshape(2, seq, head, rows, LANES), w_key, w_value)
    return attended[None], d_query[None], d_states[None]


def solution(mesh):
    sizes = mesh.shape
    return jax.shard_map(
        functools.partial(on_device, sizes["grp"], sizes["seq"], sizes["head"]),
        mesh=mesh,
        in_specs=(
            P("grp", ("seq", "head"), None),
            P(),
            P(),
            P("grp", "seq", "head"),
            P("grp", "seq", "head"),
            P("grp"),
            P("grp"),
        ),
        out_specs=(
            P("grp", "seq", "head"),
            P("grp", "seq", "head"),
            P("grp", ("seq", "head"), None),
        ),
        check_vma=False,
    )
```

```python
import functools

import jax
import jax.numpy as jnp
from jax import lax
from jax.experimental import pallas as pl
from jax.experimental.pallas import tpu as pltpu
from jax.sharding import PartitionSpec as P

HDIM = 64
LANES = 128
SCALE = HDIM ** (-0.5)
FRAME_UNIT = 256
FRAME_SIZES = (4, 2, 1)
TOKEN_TILE = 512
BF16 = jnp.bfloat16
F32 = jnp.float32
VMEM = pltpu.VMEM
MIB = 1 << 20


def dot(a, b):
    return jnp.dot(a, b, preferred_element_type=F32)


def dot_t(a, b):
    return lax.dot_general(a, b, (((1,), (1,)), ((), ())), preferred_element_type=F32)


def decompose(count, unit, sizes, fn):
    big = sizes[0]

    def step(i, _):
        fn(pl.multiple_of(i * (big * unit), big * unit), big * unit)
        return 0

    whole = count // big
    lax.fori_loop(0, whole, step, 0)
    start = whole * big
    for size in sizes[1:]:
        has = (count & size) != 0

        @pl.when(has)
        def _(start=start, size=size):
            fn(pl.multiple_of(start * unit, size * unit), size * unit)

        start = start + jnp.where(has, size, 0)


def params(mib):
    return pltpu.CompilerParams(vmem_limit_bytes=mib * MIB)


def cost(us):
    return pl.CostEstimate(flops=int(us * 1.1e9), bytes_accessed=int(us * 3e6), transcendentals=0)


def vmem_spec(count):
    return [pl.BlockSpec(memory_space=VMEM)] * count


def smem_spec():
    return pl.BlockSpec(memory_space=pltpu.SMEM)


def pack_kernel(lim_ref, q_ref, g_ref, own_ref, pair_ref):
    tok = q_ref.shape[0]
    row = lax.broadcasted_iota(jnp.int32, (tok, LANES), 0)
    q = q_ref[...].astype(F32) * SCALE
    g = jnp.where(row < lim_ref[0], g_ref[...].astype(F32), 0.0)
    low = jnp.concatenate([q[:, :HDIM], g[:, :HDIM]], axis=1)
    high = jnp.concatenate([q[:, HDIM:], g[:, HDIM:]], axis=1)
    first = lim_ref[1] == 0
    own_ref[...] = jnp.where(first, low, high).astype(BF16)
    pair_ref[...] = jnp.where(first, high, low).astype(BF16)


def pack(lim, q, g):
    shape = jax.ShapeDtypeStruct(q.shape, BF16)
    return pl.pallas_call(
        pack_kernel,
        in_specs=[smem_spec()] + vmem_spec(2),
        out_specs=vmem_spec(2),
        out_shape=[shape, shape],
        compiler_params=params(40),
        cost_estimate=cost(0.7),
        name="pack",
    )(lim, q, g)


def project_kernel(x_ref, wk_ref, wv_ref, out_ref):
    parts, rows = out_ref.shape[1], out_ref.shape[3]
    w = jnp.concatenate([wk_ref[...], wv_ref[...]], axis=1)
    kv = dot(x_ref[...], w).astype(BF16)
    k, v = kv[:, :LANES], kv[:, LANES:]
    for g in range(2):
        cols = slice(g * HDIM, (g + 1) * HDIM)
        both = jnp.concatenate([k[:, cols], v[:, cols]], axis=1)
        out_ref[g, :, 0] = both.reshape(parts, rows, LANES)


def project(x, wk, wv, seq, head):
    frames, depth = x.shape
    rows = frames // seq
    return pl.pallas_call(
        project_kernel,
        grid=(head,),
        in_specs=[
            pl.BlockSpec((frames, depth), lambda i: (0, 0)),
            pl.BlockSpec((depth, LANES), lambda i: (0, i)),
            pl.BlockSpec((depth, LANES), lambda i: (0, i)),
        ],
        out_specs=pl.BlockSpec((2, seq, 1, rows, LANES), lambda i: (0, 0, i, 0, 0)),
        out_shape=jax.ShapeDtypeStruct((2, seq, head, rows, LANES), BF16),
        compiler_params=params(40),
        cost_estimate=cost(6),
        name="project",
    )(x, wk, wv)


def load_frames(n, kv_ref, r, kvx_ref, kt_ref, which):
    size = 2 * FRAME_UNIT
    first = kv_ref[r, 0:1, :].astype(F32)

    def step(i, _):
        at = pl.multiple_of(i * size, size)
        rows = pl.ds(at, size)
        blk = kv_ref[r, rows, :]
        row = lax.broadcasted_iota(jnp.int32, (size, LANES), 0) + at
        kvx_ref[rows, :] = jnp.where(row < n, blk.astype(F32), first).astype(BF16)
        t = jnp.transpose(blk)[which * HDIM : (which + 1) * HDIM]
        col = lax.broadcasted_iota(jnp.int32, (HDIM, size), 1) + at
        kt_ref[0:HDIM, rows] = jnp.where(col < n, t.astype(F32), 0.0).astype(BF16)
        if which == 1:
            sub = lax.broadcasted_iota(jnp.int32, (16, size), 0)
            col = lax.broadcasted_iota(jnp.int32, (16, size), 1) + at
            ones = jnp.where((sub == 0) & (col < n), 1.0, 0.0)
            kt_ref[HDIM : HDIM + 16, rows] = ones.astype(BF16)
        return 0

    lax.fori_loop(0, pl.cdiv(n, size), step, 0)


def load_tokens(limit, x_ref, r, store):
    tok = x_ref.shape[2]

    def step(b, _):
        store(pl.multiple_of(b * tok, tok), x_ref[b, r])
        return 0

    lax.fori_loop(0, pl.cdiv(limit, tok), step, 0)


def forward_kernel(lim_ref, kv_ref, x_ref, o_ref, st_ref, kvx_ref, vt_ref, qt_ref, gt_ref, m_ref, acc_ref):
    tok = x_ref.shape[2]
    tile = min(TOKEN_TILE, tok)

    def store(at, blk):
        t = jnp.transpose(blk)
        qt_ref[:, pl.ds(at, tok)] = jnp.concatenate([t[:HDIM], jnp.zeros((HDIM, tok), BF16)], axis=0)
        gt_ref[:, pl.ds(at, tok)] = t[HDIM:]

    o_ref[...] = jnp.zeros_like(o_ref)
    st_ref[...] = jnp.zeros_like(st_ref)
    for r in range(2):
        n, limit = lim_ref[r], lim_ref[2 + r]
        load_tokens(limit, x_ref, r, store)
        load_frames(n, kv_ref, lim_ref[6] ^ r, kvx_ref, vt_ref, 1)

        def tokens(tt, _, r=r, n=n, limit=limit):
            at = pl.multiple_of(tt * tile, tile)
            m_ref[...] = jnp.full(m_ref.shape, -3e38, F32)
            acc_ref[...] = jnp.zeros_like(acc_ref)

            q = qt_ref[:, pl.ds(at, tile)]

            def step(fat, size):
                s = dot(kvx_ref[pl.ds(fat, size), :], q)
                old = m_ref[0:1, :]
                new = jnp.maximum(old, jnp.max(s, axis=0, keepdims=True))
                p = jnp.exp(s - new).astype(BF16)
                acc_ref[...] = acc_ref[...] * jnp.exp(old - new) + dot(vt_ref[:, pl.ds(fat, size)], p)
                m_ref[0:1, :] = new

            decompose(pl.cdiv(n, FRAME_UNIT), FRAME_UNIT, FRAME_SIZES, step)
            total = acc_ref[HDIM : HDIM + 1, :]
            o = acc_ref[0:HDIM, :] * (1.0 / total)
            g = gt_ref[:, pl.ds(at, tile)].astype(F32)
            col = lax.broadcasted_iota(jnp.int32, (HDIM, tile), 1) + at
            cols = pl.ds(pl.multiple_of(lax.rem(at, tok), tile), tile)
            o_ref[at // tok, r, :, cols] = jnp.where(col < limit, o, 0.0)
            st_ref[r : r + 1, pl.ds(at, tile)] = m_ref[0:1, :] + jnp.log(total)
            st_ref[2 + r : 3 + r, pl.ds(at, tile)] = jnp.sum(o * g, axis=0, keepdims=True)
            return 0

        lax.fori_loop(0, pl.cdiv(limit, tile), tokens, 0)


def forward(lim, kv, x):
    count, _, tok, _ = x.shape
    length = tok * count
    frames = kv.shape[1]
    return pl.pallas_call(
        forward_kernel,
        in_specs=[smem_spec()] + vmem_spec(2),
        out_specs=vmem_spec(2),
        out_shape=[
            jax.ShapeDtypeStruct((count, 2, HDIM, tok), F32),
            jax.ShapeDtypeStruct((4, length), F32),
        ],
        scratch_shapes=[
            VMEM((frames, LANES), BF16),
            VMEM((HDIM + 16, frames), BF16),
            VMEM((LANES, length), BF16),
            VMEM((HDIM, length), BF16),
            VMEM((8, min(TOKEN_TILE, tok)), F32),
            VMEM((HDIM + 16, min(TOKEN_TILE, tok)), F32),
        ],
        compiler_params=params(48),
        cost_estimate=cost(30),
        name="forward",
    )(lim, kv, x)


def combine_kernel(count, o_ref, *refs):
    st_refs = refs[:count]
    out_ref, stat_ref = refs[count:]
    tok = o_ref.shape[3]
    for r in range(2):
        tops = [st[r : r + 1, :] for st in st_refs]
        top = functools.reduce(jnp.maximum, tops)
        weights = [jnp.exp(t - top) for t in tops]
        total = functools.reduce(jnp.add, weights)
        inverse = 1.0 / total
        delta = functools.reduce(jnp.add, [w * st[2 + r : 3 + r, :] for w, st in zip(weights, st_refs)])
        stat_ref[r : r + 1, :] = top + jnp.log(total)
        stat_ref[2 + r : 3 + r, :] = delta * inverse
        mine = weights[0] * inverse
        for b in range(o_ref.shape[0]):
            out_ref[b, r] = (o_ref[b, r] * mine[:, b * tok : (b + 1) * tok]).astype(BF16)


def combine(o, stats):
    count = len(stats)
    return pl.pallas_call(
        functools.partial(combine_kernel, count),
        in_specs=vmem_spec(1 + count),
        out_specs=vmem_spec(2),
        out_shape=[
            jax.ShapeDtypeStruct(o.shape, BF16),
            jax.ShapeDtypeStruct(stats[0].shape, F32),
        ],
        compiler_params=params(40),
        cost_estimate=cost(2),
        name="combine",
    )(o, *stats)


def backward_kernel(lim_ref, kv_ref, stat_ref, x_ref, dkv_ref, keep_ref, send_ref, *refs):
    kvx_ref, kt_ref, qt_ref, gt_ref, q_ref, g_ref, dq_acc, dkv_acc = refs
    tok = x_ref.shape[2]
    tile = min(TOKEN_TILE, tok)

    def store(at, blk):
        t = jnp.transpose(blk)
        zero = jnp.zeros((HDIM, tok), BF16)
        qt_ref[:, pl.ds(at, tok)] = jnp.concatenate([t[:HDIM], zero], axis=0)
        gt_ref[:, pl.ds(at, tok)] = jnp.concatenate([zero, t[HDIM:]], axis=0)
        lane = lax.broadcasted_iota(jnp.int32, (tok, LANES), 1)
        wide = blk.astype(F32)
        q_ref[pl.ds(at, tok), :] = jnp.where(lane < HDIM, wide, 0.0).astype(BF16)
        g_ref[pl.ds(at, tok), :] = jnp.where(lane < HDIM, 0.0, wide).astype(BF16)

    dkv_ref[...] = jnp.zeros_like(dkv_ref)
    for r in range(2):
        n, limit = lim_ref[r], lim_ref[2 + r]
        load_tokens(limit, x_ref, r, store)
        rec = lim_ref[6] ^ r
        load_frames(n, kv_ref, rec, kvx_ref, kt_ref, 0)
        dq_acc[...] = jnp.zeros_like(dq_acc)
        n_t = pl.cdiv(limit, tile)

        def blocks(fat, size, r=r, rec=rec, n=n, n_t=n_t):
            dkv_acc[0:size, :] = jnp.zeros((size, LANES), F32)

            def step(tt, _):
                at = pl.multiple_of(tt * tile, tile)
                rows = pl.ds(at, tile)
                kv = kvx_ref[pl.ds(fat, size), :]
                s = dot(kv, qt_ref[:, rows])
                dp = dot(kv, gt_ref[:, rows])
                p = jnp.exp(s - stat_ref[r : r + 1, rows])
                ds = (p * (dp - stat_ref[2 + r : 3 + r, rows])).astype(BF16)
                dq_acc[:, rows] += dot(kt_ref[:, pl.ds(fat, size)], ds)
                left = jnp.concatenate([ds, p.astype(BF16)], axis=1)
                right = jnp.concatenate([q_ref[rows, :], g_ref[rows, :]], axis=0)
                dkv_acc[0:size, :] += dot(left, right)
                return 0

            lax.fori_loop(0, n_t, step, 0)
            row = lax.broadcasted_iota(jnp.int32, (size, LANES), 0) + fat
            dkv_ref[rec, pl.ds(fat, size), :] = jnp.where(row < n, dkv_acc[0:size, :], 0.0).astype(BF16)

        decompose(pl.cdiv(n, FRAME_UNIT), FRAME_UNIT, FRAME_SIZES, blocks)
        for c in range(x_ref.shape[0] // 2):
            even = dq_acc[:, (2 * c) * tok : (2 * c + 1) * tok] * SCALE
            odd = dq_acc[:, (2 * c + 1) * tok : (2 * c + 2) * tok] * SCALE
            first = lim_ref[4] == 0
            keep_ref[c, r] = jnp.where(first, even, odd)
            send_ref[c, r] = jnp.where(first, odd, even).astype(BF16)


def backward(lim, kv, stat, x):
    count, _, tok, _ = x.shape
    length = tok * count
    frames = kv.shape[1]
    return pl.pallas_call(
        backward_kernel,
        in_specs=[smem_spec()] + vmem_spec(3),
        out_specs=vmem_spec(3),
        out_shape=[
            jax.ShapeDtypeStruct(kv.shape, BF16),
            jax.ShapeDtypeStruct((count // 2, 2, HDIM, tok), F32),
            jax.ShapeDtypeStruct((count // 2, 2, HDIM, tok), BF16),
        ],
        scratch_shapes=[
            VMEM((frames, LANES), BF16),
            VMEM((HDIM, frames), BF16),
            VMEM((LANES, length), BF16),
            VMEM((LANES, length), BF16),
            VMEM((length, LANES), BF16),
            VMEM((length, LANES), BF16),
            VMEM((HDIM, length), F32),
            VMEM((FRAME_UNIT * FRAME_SIZES[0], LANES), F32),
        ],
        compiler_params=params(48),
        cost_estimate=cost(40),
        name="backward",
    )(lim, kv, stat, x)


def pair_kernel(lim_ref, keep_ref, got_ref, *outs):
    for i, out in enumerate(outs):
        chip = lim_ref[5] ^ i
        out[...] = (keep_ref[chip] + got_ref[chip].astype(F32)).astype(BF16)


def add_pair(lim, keep, got):
    shape = jax.ShapeDtypeStruct(keep.shape[1:], BF16)
    return pl.pallas_call(
        pair_kernel,
        in_specs=[smem_spec()] + vmem_spec(2),
        out_specs=vmem_spec(keep.shape[0]),
        out_shape=[shape] * keep.shape[0],
        compiler_params=params(40),
        cost_estimate=cost(1),
        name="add_pair",
    )(lim, keep, got)


def sum_kernel(count, *refs):
    own_ref, other_ref = refs[count:]
    total = functools.reduce(jnp.add, [x[...].astype(F32) for x in refs[:count]])
    own_ref[...] = total[0]
    other_ref[...] = total[1].astype(BF16)


def sum_parts(parts):
    shape = parts[0].shape[1:]
    return pl.pallas_call(
        functools.partial(sum_kernel, len(parts)),
        in_specs=vmem_spec(len(parts)),
        out_specs=vmem_spec(2),
        out_shape=[jax.ShapeDtypeStruct(shape, F32), jax.ShapeDtypeStruct(shape, BF16)],
        compiler_params=params(40),
        cost_estimate=cost(1),
        name="sum_parts",
    )(*parts)


def join_kernel(lim_ref, own_ref, got_ref, out_ref):
    a, b = own_ref[...].astype(F32), got_ref[...].astype(F32)
    first = lim_ref[6] == 0
    both = jnp.concatenate([jnp.where(first, a, b), jnp.where(first, b, a)], axis=0)
    out_ref[...] = jnp.transpose(both).astype(BF16)


def join(lim, own, got):
    return pl.pallas_call(
        join_kernel,
        in_specs=[smem_spec()] + vmem_spec(2),
        out_specs=pl.BlockSpec(memory_space=VMEM),
        out_shape=jax.ShapeDtypeStruct((own.shape[1], LANES), BF16),
        compiler_params=params(40),
        cost_estimate=cost(1),
        name="join",
    )(lim, own, got)


def encoder_kernel(d_ref, wk_ref, wv_ref, out_ref, left_ref):
    heads = d_ref.shape[2]
    rows = d_ref.shape[1] * d_ref.shape[3]
    width = heads * LANES

    @pl.when(pl.program_id(0) == 0)
    def _():
        for h in range(heads):
            a = d_ref[0, :, h].reshape(rows, LANES)
            b = d_ref[1, :, h].reshape(rows, LANES)
            left_ref[:, h * LANES : (h + 1) * LANES] = jnp.concatenate([a[:, :HDIM], b[:, :HDIM]], axis=1)
            at = width + h * LANES
            left_ref[:, at : at + LANES] = jnp.concatenate([a[:, HDIM:], b[:, HDIM:]], axis=1)

    right = jnp.concatenate([wk_ref[...], wv_ref[...]], axis=1)
    out_ref[...] = dot_t(left_ref[...], right).astype(BF16)


def encoder_grad(d, wk, wv):
    rows = d.shape[1] * d.shape[3]
    depth, width = wk.shape
    tile = 256
    return pl.pallas_call(
        encoder_kernel,
        grid=(depth // tile,),
        in_specs=[
            pl.BlockSpec(d.shape, lambda i: (0, 0, 0, 0, 0)),
            pl.BlockSpec((tile, width), lambda i: (i, 0)),
            pl.BlockSpec((tile, width), lambda i: (i, 0)),
        ],
        out_specs=pl.BlockSpec((rows, tile), lambda i: (0, i)),
        out_shape=jax.ShapeDtypeStruct((rows, depth), BF16),
        scratch_shapes=[VMEM((rows, 2 * width), BF16)],
        compiler_params=params(40),
        cost_estimate=cost(4),
        name="encoder_grad",
    )(d, wk, wv)


def on_device(grp, seq, head, encoder, w_key, w_value, queries, d_out, n_frames, t_len):
    every = ("grp", "seq", "head")
    me_g, me_s = lax.axis_index("grp"), lax.axis_index("seq")
    chips = seq // 2

    def away(x, i):
        return x if i == 0 else lax.ppermute(x, "seq", [(s, s ^ (2 * i)) for s in range(seq)])

    def to_pair(x):
        return lax.ppermute(x, "seq", [(s, s ^ 1) for s in range(seq)])

    def to_other(x):
        return lax.ppermute(x, "grp", [(0, 1), (1, 0)])

    tok = queries.shape[1]
    frames = encoder.shape[1]
    rows = frames // seq
    own, pair = pack(jnp.stack([t_len[0] - me_s * tok, me_g]), queries[0], d_out[0])
    both = jnp.stack([own, to_other(pair)])
    states, both = lax.optimization_barrier((encoder[0], both))
    x = lax.all_gather(both, "seq", axis=0, tiled=False)

    bounds = jnp.concatenate([n_frames, t_len])
    bounds = jnp.stack([bounds, to_other(bounds)])
    n = bounds[:, 0]
    here = (n // frames) * rows + jnp.clip(n % frames - rows * me_s, 0, rows)
    lim = jnp.concatenate([here, bounds[:, 1], jnp.stack([me_s % 2, me_s // 2, me_g])]).astype(jnp.int32)

    kv = project(states, w_key, w_value, seq, head)
    kv = lax.all_to_all(kv.reshape(grp * seq * head, rows, LANES), every, 0, 0, tiled=True)
    kv = kv.reshape(2, seq * head * rows, LANES)

    o_part, local = forward(lim, kv, x)
    local = [away(local, i) for i in range(chips)]
    o_part, stat = combine(o_part, local + [to_pair(p) for p in local])
    o_sum = lax.psum_scatter(o_part, "seq", scatter_dimension=0, tiled=False)
    d_kv, keep, send = backward(lim, kv, stat, x)
    got = to_pair(send)
    d_kv = lax.all_to_all(d_kv.reshape(grp * seq * head, rows, LANES), every, 0, 0, tiled=True)
    parts = [away(p, i) for i, p in enumerate(add_pair(lim, keep, got))]
    attended = join(lim, o_sum[0], to_other(o_sum[1]))
    parts, attended = lax.optimization_barrier((parts, attended))
    dq_own, dq_other = sum_parts(parts)
    dq_other = to_other(dq_other)
    d_states = encoder_grad(d_kv.reshape(2, seq, head, rows, LANES), w_key, w_value)
    dq_own, d_states = lax.optimization_barrier((dq_own, d_states))
    d_query = join(lim, dq_own, dq_other)
    return attended[None], d_query[None], d_states[None]


def solution(mesh):
    sizes = mesh.shape
    return jax.shard_map(
        functools.partial(on_device, sizes["grp"], sizes["seq"], sizes["head"]),
        mesh=mesh,
        in_specs=(
            P("grp", ("seq", "head"), None),
            P(),
            P(),
            P("grp", "seq", "head"),
            P("grp", "seq", "head"),
            P("grp"),
            P("grp"),
        ),
        out_specs=(
            P("grp", "seq", "head"),
            P("grp", "seq", "head"),
            P("grp", ("seq", "head"), None),
        ),
        check_vma=False,
    )
```

```python
import functools

import jax
import jax.numpy as jnp
from jax import lax
from jax.experimental import pallas as pl
from jax.experimental.pallas import tpu as pltpu
from jax.sharding import PartitionSpec as P

HDIM = 64
LANES = 128
SCALE = HDIM ** (-0.5)
FRAME_UNIT = 256
FRAME_SIZES = (4, 2, 1)
TOKEN_TILE = 512
FORWARD_TILES = (4, 2, 1)
BACKWARD_TILES = (2, 1)
BF16 = jnp.bfloat16
F32 = jnp.float32
VMEM = pltpu.VMEM
MIB = 1 << 20


def dot(a, b):
    return jnp.dot(a, b, preferred_element_type=F32)


def dot_t(a, b):
    return lax.dot_general(a, b, (((1,), (1,)), ((), ())), preferred_element_type=F32)


def decompose(count, unit, sizes, fn):
    big = sizes[0]

    def step(i, _):
        fn(pl.multiple_of(i * (big * unit), big * unit), big * unit)
        return 0

    whole = count // big
    lax.fori_loop(0, whole, step, 0)
    start = whole * big
    for size in sizes[1:]:
        has = (count & size) != 0

        @pl.when(has)
        def _(start=start, size=size):
            fn(pl.multiple_of(start * unit, size * unit), size * unit)

        start = start + jnp.where(has, size, 0)


def params(mib):
    return pltpu.CompilerParams(vmem_limit_bytes=mib * MIB)


def cost(us):
    return pl.CostEstimate(flops=int(us * 1.1e9), bytes_accessed=int(us * 3e6), transcendentals=0)


def vmem_spec(count):
    return [pl.BlockSpec(memory_space=VMEM)] * count


def smem_spec():
    return pl.BlockSpec(memory_space=pltpu.SMEM)


def pack_kernel(lim_ref, q_ref, g_ref, own_ref, pair_ref):
    tok = q_ref.shape[0]
    row = lax.broadcasted_iota(jnp.int32, (tok, LANES), 0)
    q = q_ref[...].astype(F32) * SCALE
    g = jnp.where(row < lim_ref[0], g_ref[...].astype(F32), 0.0)
    low = jnp.concatenate([q[:, :HDIM], g[:, :HDIM]], axis=1)
    high = jnp.concatenate([q[:, HDIM:], g[:, HDIM:]], axis=1)
    first = lim_ref[1] == 0
    own_ref[...] = jnp.where(first, low, high).astype(BF16)
    pair_ref[...] = jnp.where(first, high, low).astype(BF16)


def pack(lim, q, g):
    shape = jax.ShapeDtypeStruct(q.shape, BF16)
    return pl.pallas_call(
        pack_kernel,
        in_specs=[smem_spec()] + vmem_spec(2),
        out_specs=vmem_spec(2),
        out_shape=[shape, shape],
        compiler_params=params(4),
        cost_estimate=cost(0.7),
        name="pack",
    )(lim, q, g)


def project_kernel(x_ref, wk_ref, wv_ref, out_ref):
    parts, heads, rows = out_ref.shape[1:4]
    step = 2 if heads % 2 == 0 else 1
    for at in range(0, heads, step):
        cols = slice(at * LANES, (at + step) * LANES)
        k = dot(x_ref[...], wk_ref[:, cols]).astype(BF16)
        v = dot(x_ref[...], wv_ref[:, cols]).astype(BF16)
        for h in range(step):
            for g in range(2):
                mine = slice(h * LANES + g * HDIM, h * LANES + (g + 1) * HDIM)
                both = jnp.concatenate([k[:, mine], v[:, mine]], axis=1)
                out_ref[g, :, at + h] = both.reshape(parts, rows, LANES)


def project(x, wk, wv, seq, head):
    return pl.pallas_call(
        project_kernel,
        in_specs=vmem_spec(3),
        out_specs=pl.BlockSpec(memory_space=VMEM),
        out_shape=jax.ShapeDtypeStruct((2, seq, head, x.shape[0] // seq, LANES), BF16),
        compiler_params=params(10),
        cost_estimate=cost(4),
        name="project",
    )(x, wk, wv)


def load_frames(n, kv_ref, r, kvx_ref, kt_ref, which):
    size = 2 * FRAME_UNIT
    first = kv_ref[r, 0:1, :].astype(F32)

    def step(i, _):
        at = pl.multiple_of(i * size, size)
        rows = pl.ds(at, size)
        blk = kv_ref[r, rows, :]
        row = lax.broadcasted_iota(jnp.int32, (size, LANES), 0) + at
        kvx_ref[rows, :] = jnp.where(row < n, blk.astype(F32), first).astype(BF16)
        t = jnp.transpose(blk)[which * HDIM : (which + 1) * HDIM]
        col = lax.broadcasted_iota(jnp.int32, (HDIM, size), 1) + at
        kt_ref[0:HDIM, rows] = jnp.where(col < n, t.astype(F32), 0.0).astype(BF16)
        if which == 1:
            sub = lax.broadcasted_iota(jnp.int32, (16, size), 0)
            col = lax.broadcasted_iota(jnp.int32, (16, size), 1) + at
            ones = jnp.where((sub == 0) & (col < n), 1.0, 0.0)
            kt_ref[HDIM : HDIM + 16, rows] = ones.astype(BF16)
        return 0

    lax.fori_loop(0, pl.cdiv(n, size), step, 0)


def load_tokens(limit, x_ref, r, store):
    tok = x_ref.shape[2]

    def step(b, _):
        store(pl.multiple_of(b * tok, tok), x_ref[b, r])
        return 0

    lax.fori_loop(0, pl.cdiv(limit, tok), step, 0)


def forward_kernel(lim_ref, kv_ref, x_ref, o_ref, st_ref, kvx_ref, vt_ref, qt_ref, gt_ref, m_ref, acc_ref):
    tok = x_ref.shape[2]
    tile = min(TOKEN_TILE, tok)

    def store(at, blk):
        t = jnp.transpose(blk)
        qt_ref[:, pl.ds(at, tok)] = jnp.concatenate([t[:HDIM], jnp.zeros((HDIM, tok), BF16)], axis=0)
        gt_ref[:, pl.ds(at, tok)] = t[HDIM:]

    o_ref[...] = jnp.zeros_like(o_ref)
    st_ref[...] = jnp.zeros_like(st_ref)
    for r in range(2):
        n, limit = lim_ref[r], lim_ref[2 + r]
        load_tokens(limit, x_ref, r, store)
        load_frames(n, kv_ref, lim_ref[6] ^ r, kvx_ref, vt_ref, 1)

        def tokens(at, size, r=r, n=n, limit=limit):
            cuts = [slice(c, c + tile) for c in range(0, size, tile)]
            m_ref[...] = jnp.full(m_ref.shape, -3e38, F32)
            acc_ref[...] = jnp.zeros_like(acc_ref)

            def step(fat, depth):
                rows = pl.ds(fat, depth)
                ss = [dot(kvx_ref[rows, :], qt_ref[:, pl.ds(at + i * tile, tile)]) for i in range(len(cuts))]
                olds = [m_ref[0:1, cut] for cut in cuts]
                news = [jnp.maximum(o, jnp.max(x, axis=0, keepdims=True)) for o, x in zip(olds, ss)]
                ps = [jnp.exp(x - n1).astype(BF16) for x, n1 in zip(ss, news)]
                for cut, o, n1, p in zip(cuts, olds, news, ps):
                    acc_ref[:, cut] = acc_ref[:, cut] * jnp.exp(o - n1) + dot(vt_ref[:, rows], p)
                    m_ref[0:1, cut] = n1

            decompose(pl.cdiv(n, FRAME_UNIT), FRAME_UNIT, FRAME_SIZES, step)
            for i, cut in enumerate(cuts):
                here = pl.multiple_of(at + i * tile, tile)
                total = acc_ref[HDIM : HDIM + 1, cut]
                o = acc_ref[0:HDIM, cut] * (1.0 / total)
                g = gt_ref[:, pl.ds(here, tile)].astype(F32)
                col = lax.broadcasted_iota(jnp.int32, (HDIM, tile), 1) + here
                cols = pl.ds(pl.multiple_of(lax.rem(here, tok), tile), tile)
                o_ref[here // tok, r, :, cols] = jnp.where(col < limit, o, 0.0)
                st_ref[r : r + 1, pl.ds(here, tile)] = m_ref[0:1, cut] + jnp.log(total)
                st_ref[2 + r : 3 + r, pl.ds(here, tile)] = jnp.sum(o * g, axis=0, keepdims=True)

        decompose(pl.cdiv(limit, tile), tile, FORWARD_TILES, tokens)


def forward(lim, kv, x):
    count, _, tok, _ = x.shape
    length = tok * count
    frames = kv.shape[1]
    return pl.pallas_call(
        forward_kernel,
        in_specs=[smem_spec()] + vmem_spec(2),
        out_specs=vmem_spec(2),
        out_shape=[
            jax.ShapeDtypeStruct((count, 2, HDIM, tok), F32),
            jax.ShapeDtypeStruct((4, length), F32),
        ],
        scratch_shapes=[
            VMEM((frames, LANES), BF16),
            VMEM((HDIM + 16, frames), BF16),
            VMEM((LANES, length), BF16),
            VMEM((HDIM, length), BF16),
            VMEM((8, FORWARD_TILES[0] * min(TOKEN_TILE, tok)), F32),
            VMEM((HDIM + 16, FORWARD_TILES[0] * min(TOKEN_TILE, tok)), F32),
        ],
        compiler_params=params(26),
        cost_estimate=cost(30),
        name="forward",
    )(lim, kv, x)


def combine_kernel(count, o_ref, *refs):
    st_refs = refs[:count]
    out_ref, stat_ref = refs[count:]
    tok = o_ref.shape[3]
    for r in range(2):
        tops = [st[r : r + 1, :] for st in st_refs]
        top = functools.reduce(jnp.maximum, tops)
        weights = [jnp.exp(t - top) for t in tops]
        total = functools.reduce(jnp.add, weights)
        inverse = 1.0 / total
        delta = functools.reduce(jnp.add, [w * st[2 + r : 3 + r, :] for w, st in zip(weights, st_refs)])
        stat_ref[r : r + 1, :] = top + jnp.log(total)
        stat_ref[2 + r : 3 + r, :] = delta * inverse
        mine = weights[0] * inverse
        for b in range(o_ref.shape[0]):
            out_ref[b, r] = (o_ref[b, r] * mine[:, b * tok : (b + 1) * tok]).astype(BF16)


def combine(o, stats):
    count = len(stats)
    return pl.pallas_call(
        functools.partial(combine_kernel, count),
        in_specs=vmem_spec(1 + count),
        out_specs=vmem_spec(2),
        out_shape=[
            jax.ShapeDtypeStruct(o.shape, BF16),
            jax.ShapeDtypeStruct(stats[0].shape, F32),
        ],
        compiler_params=params(10),
        cost_estimate=cost(2),
        name="combine",
    )(o, *stats)


def backward_kernel(lim_ref, kv_ref, stat_ref, x_ref, dkv_ref, keep_ref, send_ref, *refs):
    kvx_ref, kt_ref, qt_ref, gt_ref, q_ref, g_ref, dq_acc, dkv_acc = refs
    tok = x_ref.shape[2]
    tile = min(TOKEN_TILE, tok)

    def store(at, blk):
        t = jnp.transpose(blk)
        zero = jnp.zeros((HDIM, tok), BF16)
        qt_ref[:, pl.ds(at, tok)] = jnp.concatenate([t[:HDIM], zero], axis=0)
        gt_ref[:, pl.ds(at, tok)] = jnp.concatenate([zero, t[HDIM:]], axis=0)
        lane = lax.broadcasted_iota(jnp.int32, (tok, LANES), 1)
        wide = blk.astype(F32)
        q_ref[pl.ds(at, tok), :] = jnp.where(lane < HDIM, wide, 0.0).astype(BF16)
        g_ref[pl.ds(at, tok), :] = jnp.where(lane < HDIM, 0.0, wide).astype(BF16)

    dkv_ref[...] = jnp.zeros_like(dkv_ref)
    for r in range(2):
        n, limit = lim_ref[r], lim_ref[2 + r]
        load_tokens(limit, x_ref, r, store)
        rec = lim_ref[6] ^ r
        load_frames(n, kv_ref, rec, kvx_ref, kt_ref, 0)
        dq_acc[...] = jnp.zeros_like(dq_acc)
        n_t = pl.cdiv(limit, tile)

        def blocks(fat, size, r=r, rec=rec, n=n, n_t=n_t):
            dkv_acc[0:size, :] = jnp.zeros((size, LANES), F32)

            def step(at, width):
                kv = kvx_ref[pl.ds(fat, size), :]
                rows = [pl.ds(at + c, tile) for c in range(0, width, tile)]
                ss = [(dot(kv, qt_ref[:, c]), dot(kv, gt_ref[:, c])) for c in rows]
                ps = [jnp.exp(s - stat_ref[r : r + 1, c]) for c, (s, _) in zip(rows, ss)]
                ds = [(p * (dp - stat_ref[2 + r : 3 + r, c])).astype(BF16) for c, p, (_, dp) in zip(rows, ps, ss)]
                for c, d in zip(rows, ds):
                    dq_acc[:, c] += dot(kt_ref[:, pl.ds(fat, size)], d)
                left = jnp.concatenate(ds + [p.astype(BF16) for p in ps], axis=1)
                right = jnp.concatenate([x[c, :] for x in (q_ref, g_ref) for c in rows], axis=0)
                dkv_acc[0:size, :] += dot(left, right)

            decompose(n_t, tile, BACKWARD_TILES, step)
            row = lax.broadcasted_iota(jnp.int32, (size, LANES), 0) + fat
            dkv_ref[rec, pl.ds(fat, size), :] = jnp.where(row < n, dkv_acc[0:size, :], 0.0).astype(BF16)

        decompose(pl.cdiv(n, FRAME_UNIT), FRAME_UNIT, FRAME_SIZES, blocks)
        for c in range(x_ref.shape[0] // 2):
            even = dq_acc[:, (2 * c) * tok : (2 * c + 1) * tok] * SCALE
            odd = dq_acc[:, (2 * c + 1) * tok : (2 * c + 2) * tok] * SCALE
            first = lim_ref[4] == 0
            keep_ref[c, r] = jnp.where(first, even, odd)
            send_ref[c, r] = jnp.where(first, odd, even).astype(BF16)


def backward(lim, kv, stat, x):
    count, _, tok, _ = x.shape
    length = tok * count
    frames = kv.shape[1]
    return pl.pallas_call(
        backward_kernel,
        in_specs=[smem_spec()] + vmem_spec(3),
        out_specs=vmem_spec(3),
        out_shape=[
            jax.ShapeDtypeStruct(kv.shape, BF16),
            jax.ShapeDtypeStruct((count // 2, 2, HDIM, tok), F32),
            jax.ShapeDtypeStruct((count // 2, 2, HDIM, tok), BF16),
        ],
        scratch_shapes=[
            VMEM((frames, LANES), BF16),
            VMEM((HDIM, frames), BF16),
            VMEM((LANES, length), BF16),
            VMEM((LANES, length), BF16),
            VMEM((length, LANES), BF16),
            VMEM((length, LANES), BF16),
            VMEM((HDIM, length), F32),
            VMEM((FRAME_UNIT * FRAME_SIZES[0], LANES), F32),
        ],
        compiler_params=params(34),
        cost_estimate=cost(40),
        name="backward",
    )(lim, kv, stat, x)


def pair_kernel(lim_ref, keep_ref, got_ref, *outs):
    for i, out in enumerate(outs):
        chip = lim_ref[5] ^ i
        out[...] = (keep_ref[chip] + got_ref[chip].astype(F32)).astype(BF16)


def add_pair(lim, keep, got):
    shape = jax.ShapeDtypeStruct(keep.shape[1:], BF16)
    return pl.pallas_call(
        pair_kernel,
        in_specs=[smem_spec()] + vmem_spec(2),
        out_specs=vmem_spec(keep.shape[0]),
        out_shape=[shape] * keep.shape[0],
        compiler_params=params(4),
        cost_estimate=cost(1),
        name="add_pair",
    )(lim, keep, got)


def sum_kernel(count, *refs):
    own_ref, other_ref = refs[count:]
    total = functools.reduce(jnp.add, [x[...].astype(F32) for x in refs[:count]])
    own_ref[...] = total[0]
    other_ref[...] = total[1].astype(BF16)


def sum_parts(parts):
    shape = parts[0].shape[1:]
    return pl.pallas_call(
        functools.partial(sum_kernel, len(parts)),
        in_specs=vmem_spec(len(parts)),
        out_specs=vmem_spec(2),
        out_shape=[jax.ShapeDtypeStruct(shape, F32), jax.ShapeDtypeStruct(shape, BF16)],
        compiler_params=params(4),
        cost_estimate=cost(1),
        name="sum_parts",
    )(*parts)


def join_kernel(lim_ref, own_ref, got_ref, out_ref):
    a, b = own_ref[...].astype(F32), got_ref[...].astype(F32)
    first = lim_ref[6] == 0
    both = jnp.concatenate([jnp.where(first, a, b), jnp.where(first, b, a)], axis=0)
    out_ref[...] = jnp.transpose(both).astype(BF16)


def join(lim, own, got):
    return pl.pallas_call(
        join_kernel,
        in_specs=[smem_spec()] + vmem_spec(2),
        out_specs=pl.BlockSpec(memory_space=VMEM),
        out_shape=jax.ShapeDtypeStruct((own.shape[1], LANES), BF16),
        compiler_params=params(4),
        cost_estimate=cost(1),
        name="join",
    )(lim, own, got)


def encoder_kernel(d_ref, wk_ref, wv_ref, out_ref):
    heads = d_ref.shape[2]
    rows = d_ref.shape[1] * d_ref.shape[3]
    acc = None
    for h in range(heads):
        a = d_ref[0, :, h].reshape(rows, LANES)
        b = d_ref[1, :, h].reshape(rows, LANES)
        dk = jnp.concatenate([a[:, :HDIM], b[:, :HDIM]], axis=1)
        dv = jnp.concatenate([a[:, HDIM:], b[:, HDIM:]], axis=1)
        cols = slice(h * LANES, (h + 1) * LANES)
        left = jnp.concatenate([dk, dv], axis=1)
        right = jnp.concatenate([wk_ref[:, cols], wv_ref[:, cols]], axis=1)
        part = dot_t(left, right)
        acc = part if acc is None else acc + part
    out_ref[...] = acc.astype(BF16)


def encoder_grad(d, wk, wv):
    rows = d.shape[1] * d.shape[3]
    return pl.pallas_call(
        encoder_kernel,
        in_specs=vmem_spec(3),
        out_specs=pl.BlockSpec(memory_space=VMEM),
        out_shape=jax.ShapeDtypeStruct((rows, wk.shape[0]), BF16),
        compiler_params=params(12),
        cost_estimate=cost(4),
        name="encoder_grad",
    )(d, wk, wv)


def on_device(grp, seq, head, encoder, w_key, w_value, queries, d_out, n_frames, t_len):
    every = ("grp", "seq", "head")
    me_g, me_s = lax.axis_index("grp"), lax.axis_index("seq")
    chips = seq // 2

    def away(x, i):
        return x if i == 0 else lax.ppermute(x, "seq", [(s, s ^ (2 * i)) for s in range(seq)])

    def to_pair(x):
        return lax.ppermute(x, "seq", [(s, s ^ 1) for s in range(seq)])

    def to_other(x):
        return lax.ppermute(x, "grp", [(0, 1), (1, 0)])

    tok = queries.shape[1]
    frames = encoder.shape[1]
    rows = frames // seq
    own, pair = pack(jnp.stack([t_len[0] - me_s * tok, me_g]), queries[0], d_out[0])
    both = jnp.stack([own, to_other(pair)])
    states, both = lax.optimization_barrier((encoder[0], both))
    x = lax.all_gather(both, "seq", axis=0, tiled=False)

    bounds = jnp.concatenate([n_frames, t_len])
    bounds = jnp.stack([bounds, to_other(bounds)])
    n = bounds[:, 0]
    here = (n // frames) * rows + jnp.clip(n % frames - rows * me_s, 0, rows)
    lim = jnp.concatenate([here, bounds[:, 1], jnp.stack([me_s % 2, me_s // 2, me_g])]).astype(jnp.int32)

    kv = project(states, w_key, w_value, seq, head)
    kv = lax.all_to_all(kv.reshape(grp * seq * head, rows, LANES), every, 0, 0, tiled=True)
    kv = kv.reshape(2, seq * head * rows, LANES)

    o_part, local = forward(lim, kv, x)
    local = [away(local, i) for i in range(chips)]
    o_part, stat = combine(o_part, local + [to_pair(p) for p in local])
    o_sum = lax.psum_scatter(o_part, "seq", scatter_dimension=0, tiled=False)
    d_kv, keep, send = backward(lim, kv, stat, x)
    got = to_pair(send)
    d_kv = lax.all_to_all(d_kv.reshape(grp * seq * head, rows, LANES), every, 0, 0, tiled=True)
    parts = [away(p, i) for i, p in enumerate(add_pair(lim, keep, got))]
    attended = join(lim, o_sum[0], to_other(o_sum[1]))
    parts, attended = lax.optimization_barrier((parts, attended))
    dq_own, dq_other = sum_parts(parts)
    dq_other = to_other(dq_other)
    d_states = encoder_grad(d_kv.reshape(2, seq, head, rows, LANES), w_key, w_value)
    dq_own, d_states = lax.optimization_barrier((dq_own, d_states))
    d_query = join(lim, dq_own, dq_other)
    return attended[None], d_query[None], d_states[None]


def solution(mesh):
    sizes = mesh.shape
    return jax.shard_map(
        functools.partial(on_device, sizes["grp"], sizes["seq"], sizes["head"]),
        mesh=mesh,
        in_specs=(
            P("grp", ("seq", "head"), None),
            P(),
            P(),
            P("grp", "seq", "head"),
            P("grp", "seq", "head"),
            P("grp"),
            P("grp"),
        ),
        out_specs=(
            P("grp", "seq", "head"),
            P("grp", "seq", "head"),
            P("grp", ("seq", "head"), None),
        ),
        check_vma=False,
    )
```

```python
import functools

import jax
import jax.numpy as jnp
from jax import lax
from jax.experimental import pallas as pl
from jax.experimental.pallas import tpu as pltpu
from jax.sharding import PartitionSpec as P

HDIM = 64
LANES = 128
SCALE = HDIM ** (-0.5)
FRAME_UNIT = 256
FRAME_SIZES = (4, 2, 1)
TOKEN_TILE = 512
FORWARD_TILES = (2, 1)
BACKWARD_TILES = (2, 1)
BF16 = jnp.bfloat16
F32 = jnp.float32
VMEM = pltpu.VMEM
MIB = 1 << 20


def dot(a, b):
    return jnp.dot(a, b, preferred_element_type=F32)


def dot_t(a, b):
    return lax.dot_general(a, b, (((1,), (1,)), ((), ())), preferred_element_type=F32)


def decompose(count, unit, sizes, fn):
    big = sizes[0]

    def step(i, _):
        fn(pl.multiple_of(i * (big * unit), big * unit), big * unit)
        return 0

    whole = count // big
    lax.fori_loop(0, whole, step, 0)
    start = whole * big
    for size in sizes[1:]:
        has = (count & size) != 0

        @pl.when(has)
        def _(start=start, size=size):
            fn(pl.multiple_of(start * unit, size * unit), size * unit)

        start = start + jnp.where(has, size, 0)


def params(mib):
    return pltpu.CompilerParams(vmem_limit_bytes=mib * MIB)


def cost(us):
    return pl.CostEstimate(flops=int(us * 1.1e9), bytes_accessed=int(us * 3e6), transcendentals=0)


def vmem_spec(count):
    return [pl.BlockSpec(memory_space=VMEM)] * count


def smem_spec():
    return pl.BlockSpec(memory_space=pltpu.SMEM)


def pack_kernel(lim_ref, q_ref, g_ref, own_ref, pair_ref):
    tok = q_ref.shape[0]
    row = lax.broadcasted_iota(jnp.int32, (tok, LANES), 0)
    q = q_ref[...].astype(F32) * SCALE
    g = jnp.where(row < lim_ref[0], g_ref[...].astype(F32), 0.0)
    low = jnp.concatenate([q[:, :HDIM], g[:, :HDIM]], axis=1)
    high = jnp.concatenate([q[:, HDIM:], g[:, HDIM:]], axis=1)
    first = lim_ref[1] == 0
    own_ref[...] = jnp.where(first, low, high).astype(BF16)
    pair_ref[...] = jnp.where(first, high, low).astype(BF16)


def pack(lim, q, g):
    shape = jax.ShapeDtypeStruct(q.shape, BF16)
    return pl.pallas_call(
        pack_kernel,
        in_specs=[smem_spec()] + vmem_spec(2),
        out_specs=vmem_spec(2),
        out_shape=[shape, shape],
        compiler_params=params(4),
        cost_estimate=cost(0.7),
        name="pack",
    )(lim, q, g)


def project_kernel(x_ref, wk_ref, wv_ref, out_ref):
    parts, heads, rows = out_ref.shape[1:4]
    step = 2 if heads % 2 == 0 else 1
    for at in range(0, heads, step):
        cols = slice(at * LANES, (at + step) * LANES)
        k = dot(x_ref[...], wk_ref[:, cols]).astype(BF16)
        v = dot(x_ref[...], wv_ref[:, cols]).astype(BF16)
        for h in range(step):
            for g in range(2):
                mine = slice(h * LANES + g * HDIM, h * LANES + (g + 1) * HDIM)
                both = jnp.concatenate([k[:, mine], v[:, mine]], axis=1)
                out_ref[g, :, at + h] = both.reshape(parts, rows, LANES)


def project(x, wk, wv, seq, head):
    return pl.pallas_call(
        project_kernel,
        in_specs=vmem_spec(3),
        out_specs=pl.BlockSpec(memory_space=VMEM),
        out_shape=jax.ShapeDtypeStruct((2, seq, head, x.shape[0] // seq, LANES), BF16),
        compiler_params=params(10),
        cost_estimate=cost(4),
        name="project",
    )(x, wk, wv)


def load_frames(n, kv_ref, r, kvx_ref, kt_ref, which):
    size = 2 * FRAME_UNIT
    first = kv_ref[r, 0:1, :].astype(F32)

    def step(i, _):
        at = pl.multiple_of(i * size, size)
        rows = pl.ds(at, size)
        blk = kv_ref[r, rows, :]
        row = lax.broadcasted_iota(jnp.int32, (size, LANES), 0) + at
        kvx_ref[rows, :] = jnp.where(row < n, blk.astype(F32), first).astype(BF16)
        t = jnp.transpose(blk)[which * HDIM : (which + 1) * HDIM]
        col = lax.broadcasted_iota(jnp.int32, (HDIM, size), 1) + at
        kt_ref[0:HDIM, rows] = jnp.where(col < n, t.astype(F32), 0.0).astype(BF16)
        if which == 1:
            sub = lax.broadcasted_iota(jnp.int32, (16, size), 0)
            col = lax.broadcasted_iota(jnp.int32, (16, size), 1) + at
            ones = jnp.where((sub == 0) & (col < n), 1.0, 0.0)
            kt_ref[HDIM : HDIM + 16, rows] = ones.astype(BF16)
        return 0

    lax.fori_loop(0, pl.cdiv(n, size), step, 0)


def load_tokens(limit, x_ref, r, store):
    tok = x_ref.shape[2]

    def step(b, _):
        store(pl.multiple_of(b * tok, tok), x_ref[b, r])
        return 0

    lax.fori_loop(0, pl.cdiv(limit, tok), step, 0)


def forward_kernel(lim_ref, kv_ref, x_ref, o_ref, st_ref, kvx_ref, vt_ref, qt_ref, gt_ref, m_ref, acc_ref):
    tok = x_ref.shape[2]
    tile = min(TOKEN_TILE, tok)

    def store(at, blk):
        t = jnp.transpose(blk)
        qt_ref[:, pl.ds(at, tok)] = jnp.concatenate([t[:HDIM], jnp.zeros((HDIM, tok), BF16)], axis=0)
        gt_ref[:, pl.ds(at, tok)] = t[HDIM:]

    o_ref[...] = jnp.zeros_like(o_ref)
    st_ref[...] = jnp.zeros_like(st_ref)
    for r in range(2):
        n, limit = lim_ref[r], lim_ref[2 + r]
        load_tokens(limit, x_ref, r, store)
        load_frames(n, kv_ref, lim_ref[6] ^ r, kvx_ref, vt_ref, 1)

        def tokens(at, size, r=r, n=n, limit=limit):
            cuts = [slice(c, c + tile) for c in range(0, size, tile)]
            m_ref[...] = jnp.full(m_ref.shape, -3e38, F32)
            acc_ref[...] = jnp.zeros_like(acc_ref)

            def step(fat, depth):
                rows = pl.ds(fat, depth)
                ss = [dot(kvx_ref[rows, :], qt_ref[:, pl.ds(at + i * tile, tile)]) for i in range(len(cuts))]
                olds = [m_ref[0:1, cut] for cut in cuts]
                news = [jnp.maximum(o, jnp.max(x, axis=0, keepdims=True)) for o, x in zip(olds, ss)]
                ps = [jnp.exp(x - n1).astype(BF16) for x, n1 in zip(ss, news)]
                for cut, o, n1, p in zip(cuts, olds, news, ps):
                    acc_ref[:, cut] = acc_ref[:, cut] * jnp.exp(o - n1) + dot(vt_ref[:, rows], p)
                    m_ref[0:1, cut] = n1

            decompose(pl.cdiv(n, FRAME_UNIT), FRAME_UNIT, FRAME_SIZES, step)
            for i, cut in enumerate(cuts):
                here = pl.multiple_of(at + i * tile, tile)
                total = acc_ref[HDIM : HDIM + 1, cut]
                o = acc_ref[0:HDIM, cut] * (1.0 / total)
                g = gt_ref[:, pl.ds(here, tile)].astype(F32)
                col = lax.broadcasted_iota(jnp.int32, (HDIM, tile), 1) + here
                cols = pl.ds(pl.multiple_of(lax.rem(here, tok), tile), tile)
                o_ref[here // tok, r, :, cols] = jnp.where(col < limit, o, 0.0)
                st_ref[r : r + 1, pl.ds(here, tile)] = m_ref[0:1, cut] + jnp.log(total)
                st_ref[2 + r : 3 + r, pl.ds(here, tile)] = jnp.sum(o * g, axis=0, keepdims=True)

        decompose(pl.cdiv(limit, tile), tile, FORWARD_TILES, tokens)


def forward(lim, kv, x):
    count, _, tok, _ = x.shape
    length = tok * count
    frames = kv.shape[1]
    return pl.pallas_call(
        forward_kernel,
        in_specs=[smem_spec()] + vmem_spec(2),
        out_specs=vmem_spec(2),
        out_shape=[
            jax.ShapeDtypeStruct((count, 2, HDIM, tok), F32),
            jax.ShapeDtypeStruct((4, length), F32),
        ],
        scratch_shapes=[
            VMEM((frames, LANES), BF16),
            VMEM((HDIM + 16, frames), BF16),
            VMEM((LANES, length), BF16),
            VMEM((HDIM, length), BF16),
            VMEM((8, FORWARD_TILES[0] * min(TOKEN_TILE, tok)), F32),
            VMEM((HDIM + 16, FORWARD_TILES[0] * min(TOKEN_TILE, tok)), F32),
        ],
        compiler_params=params(26),
        cost_estimate=cost(30),
        name="forward",
    )(lim, kv, x)


def combine_kernel(count, o_ref, *refs):
    st_refs = refs[:count]
    out_ref, stat_ref = refs[count:]
    tok = o_ref.shape[3]
    for r in range(2):
        tops = [st[r : r + 1, :] for st in st_refs]
        top = functools.reduce(jnp.maximum, tops)
        weights = [jnp.exp(t - top) for t in tops]
        total = functools.reduce(jnp.add, weights)
        inverse = 1.0 / total
        delta = functools.reduce(jnp.add, [w * st[2 + r : 3 + r, :] for w, st in zip(weights, st_refs)])
        stat_ref[r : r + 1, :] = top + jnp.log(total)
        stat_ref[2 + r : 3 + r, :] = delta * inverse
        mine = weights[0] * inverse
        for b in range(o_ref.shape[0]):
            out_ref[b, r] = (o_ref[b, r] * mine[:, b * tok : (b + 1) * tok]).astype(BF16)


def combine(o, stats):
    count = len(stats)
    return pl.pallas_call(
        functools.partial(combine_kernel, count),
        in_specs=vmem_spec(1 + count),
        out_specs=vmem_spec(2),
        out_shape=[
            jax.ShapeDtypeStruct(o.shape, BF16),
            jax.ShapeDtypeStruct(stats[0].shape, F32),
        ],
        compiler_params=params(10),
        cost_estimate=cost(2),
        name="combine",
    )(o, *stats)


def backward_kernel(lim_ref, kv_ref, stat_ref, x_ref, dkv_ref, keep_ref, send_ref, *refs):
    kvx_ref, kt_ref, qt_ref, gt_ref, q_ref, g_ref, dq_acc, dkv_acc = refs
    tok = x_ref.shape[2]
    tile = min(TOKEN_TILE, tok)

    def store(at, blk):
        t = jnp.transpose(blk)
        zero = jnp.zeros((HDIM, tok), BF16)
        qt_ref[:, pl.ds(at, tok)] = jnp.concatenate([t[:HDIM], zero], axis=0)
        gt_ref[:, pl.ds(at, tok)] = jnp.concatenate([zero, t[HDIM:]], axis=0)
        lane = lax.broadcasted_iota(jnp.int32, (tok, LANES), 1)
        wide = blk.astype(F32)
        q_ref[pl.ds(at, tok), :] = jnp.where(lane < HDIM, wide, 0.0).astype(BF16)
        g_ref[pl.ds(at, tok), :] = jnp.where(lane < HDIM, 0.0, wide).astype(BF16)

    dkv_ref[...] = jnp.zeros_like(dkv_ref)
    for r in range(2):
        n, limit = lim_ref[r], lim_ref[2 + r]
        load_tokens(limit, x_ref, r, store)
        rec = lim_ref[6] ^ r
        load_frames(n, kv_ref, rec, kvx_ref, kt_ref, 0)
        dq_acc[...] = jnp.zeros_like(dq_acc)
        n_t = pl.cdiv(limit, tile)

        def blocks(fat, size, r=r, rec=rec, n=n, n_t=n_t):
            dkv_acc[0:size, :] = jnp.zeros((size, LANES), F32)

            def step(at, width):
                kv = kvx_ref[pl.ds(fat, size), :]
                rows = [pl.ds(at + c, tile) for c in range(0, width, tile)]
                ss = [(dot(kv, qt_ref[:, c]), dot(kv, gt_ref[:, c])) for c in rows]
                ps = [jnp.exp(s - stat_ref[r : r + 1, c]) for c, (s, _) in zip(rows, ss)]
                ds = [(p * (dp - stat_ref[2 + r : 3 + r, c])).astype(BF16) for c, p, (_, dp) in zip(rows, ps, ss)]
                for c, d in zip(rows, ds):
                    dq_acc[:, c] += dot(kt_ref[:, pl.ds(fat, size)], d)
                left = jnp.concatenate(ds + [p.astype(BF16) for p in ps], axis=1)
                right = jnp.concatenate([x[c, :] for x in (q_ref, g_ref) for c in rows], axis=0)
                dkv_acc[0:size, :] += dot(left, right)

            decompose(n_t, tile, BACKWARD_TILES, step)
            row = lax.broadcasted_iota(jnp.int32, (size, LANES), 0) + fat
            dkv_ref[rec, pl.ds(fat, size), :] = jnp.where(row < n, dkv_acc[0:size, :], 0.0).astype(BF16)

        decompose(pl.cdiv(n, FRAME_UNIT), FRAME_UNIT, FRAME_SIZES, blocks)
        for c in range(x_ref.shape[0] // 2):
            even = dq_acc[:, (2 * c) * tok : (2 * c + 1) * tok] * SCALE
            odd = dq_acc[:, (2 * c + 1) * tok : (2 * c + 2) * tok] * SCALE
            first = lim_ref[4] == 0
            keep_ref[c, r] = jnp.where(first, even, odd)
            send_ref[c, r] = jnp.where(first, odd, even).astype(BF16)


def backward(lim, kv, stat, x):
    count, _, tok, _ = x.shape
    length = tok * count
    frames = kv.shape[1]
    return pl.pallas_call(
        backward_kernel,
        in_specs=[smem_spec()] + vmem_spec(3),
        out_specs=vmem_spec(3),
        out_shape=[
            jax.ShapeDtypeStruct(kv.shape, BF16),
            jax.ShapeDtypeStruct((count // 2, 2, HDIM, tok), F32),
            jax.ShapeDtypeStruct((count // 2, 2, HDIM, tok), BF16),
        ],
        scratch_shapes=[
            VMEM((frames, LANES), BF16),
            VMEM((HDIM, frames), BF16),
            VMEM((LANES, length), BF16),
            VMEM((LANES, length), BF16),
            VMEM((length, LANES), BF16),
            VMEM((length, LANES), BF16),
            VMEM((HDIM, length), F32),
            VMEM((FRAME_UNIT * FRAME_SIZES[0], LANES), F32),
        ],
        compiler_params=params(34),
        cost_estimate=cost(40),
        name="backward",
    )(lim, kv, stat, x)


def pair_kernel(lim_ref, keep_ref, got_ref, *outs):
    for i, out in enumerate(outs):
        chip = lim_ref[5] ^ i
        out[...] = (keep_ref[chip] + got_ref[chip].astype(F32)).astype(BF16)


def add_pair(lim, keep, got):
    shape = jax.ShapeDtypeStruct(keep.shape[1:], BF16)
    return pl.pallas_call(
        pair_kernel,
        in_specs=[smem_spec()] + vmem_spec(2),
        out_specs=vmem_spec(keep.shape[0]),
        out_shape=[shape] * keep.shape[0],
        compiler_params=params(4),
        cost_estimate=cost(1),
        name="add_pair",
    )(lim, keep, got)


def sum_kernel(count, *refs):
    own_ref, other_ref = refs[count:]
    total = functools.reduce(jnp.add, [x[...].astype(F32) for x in refs[:count]])
    own_ref[...] = total[0]
    other_ref[...] = total[1].astype(BF16)


def sum_parts(parts):
    shape = parts[0].shape[1:]
    return pl.pallas_call(
        functools.partial(sum_kernel, len(parts)),
        in_specs=vmem_spec(len(parts)),
        out_specs=vmem_spec(2),
        out_shape=[jax.ShapeDtypeStruct(shape, F32), jax.ShapeDtypeStruct(shape, BF16)],
        compiler_params=params(4),
        cost_estimate=cost(1),
        name="sum_parts",
    )(*parts)


def join_kernel(lim_ref, own_ref, got_ref, out_ref):
    a, b = own_ref[...].astype(F32), got_ref[...].astype(F32)
    first = lim_ref[6] == 0
    both = jnp.concatenate([jnp.where(first, a, b), jnp.where(first, b, a)], axis=0)
    out_ref[...] = jnp.transpose(both).astype(BF16)


def join(lim, own, got):
    return pl.pallas_call(
        join_kernel,
        in_specs=[smem_spec()] + vmem_spec(2),
        out_specs=pl.BlockSpec(memory_space=VMEM),
        out_shape=jax.ShapeDtypeStruct((own.shape[1], LANES), BF16),
        compiler_params=params(4),
        cost_estimate=cost(1),
        name="join",
    )(lim, own, got)


def encoder_kernel(d_ref, wk_ref, wv_ref, out_ref):
    heads = d_ref.shape[2]
    rows = d_ref.shape[1] * d_ref.shape[3]
    acc = None
    for h in range(heads):
        a = d_ref[0, :, h].reshape(rows, LANES)
        b = d_ref[1, :, h].reshape(rows, LANES)
        dk = jnp.concatenate([a[:, :HDIM], b[:, :HDIM]], axis=1)
        dv = jnp.concatenate([a[:, HDIM:], b[:, HDIM:]], axis=1)
        cols = slice(h * LANES, (h + 1) * LANES)
        left = jnp.concatenate([dk, dv], axis=1)
        right = jnp.concatenate([wk_ref[:, cols], wv_ref[:, cols]], axis=1)
        part = dot_t(left, right)
        acc = part if acc is None else acc + part
    out_ref[...] = acc.astype(BF16)


def encoder_grad(d, wk, wv):
    rows = d.shape[1] * d.shape[3]
    return pl.pallas_call(
        encoder_kernel,
        in_specs=vmem_spec(3),
        out_specs=pl.BlockSpec(memory_space=VMEM),
        out_shape=jax.ShapeDtypeStruct((rows, wk.shape[0]), BF16),
        compiler_params=params(12),
        cost_estimate=cost(4),
        name="encoder_grad",
    )(d, wk, wv)


def on_device(grp, seq, head, encoder, w_key, w_value, queries, d_out, n_frames, t_len):
    every = ("grp", "seq", "head")
    me_g, me_s = lax.axis_index("grp"), lax.axis_index("seq")
    chips = seq // 2

    def away(x, i):
        return x if i == 0 else lax.ppermute(x, "seq", [(s, s ^ (2 * i)) for s in range(seq)])

    def to_pair(x):
        return lax.ppermute(x, "seq", [(s, s ^ 1) for s in range(seq)])

    def to_other(x):
        return lax.ppermute(x, "grp", [(0, 1), (1, 0)])

    tok = queries.shape[1]
    frames = encoder.shape[1]
    rows = frames // seq
    own, pair = pack(jnp.stack([t_len[0] - me_s * tok, me_g]), queries[0], d_out[0])
    both = jnp.stack([own, to_other(pair)])
    states, both = lax.optimization_barrier((encoder[0], both))
    x = lax.all_gather(both, "seq", axis=0, tiled=False)

    bounds = jnp.concatenate([n_frames, t_len])
    bounds = jnp.stack([bounds, to_other(bounds)])
    n = bounds[:, 0]
    here = (n // frames) * rows + jnp.clip(n % frames - rows * me_s, 0, rows)
    lim = jnp.concatenate([here, bounds[:, 1], jnp.stack([me_s % 2, me_s // 2, me_g])]).astype(jnp.int32)

    kv = project(states, w_key, w_value, seq, head)
    kv = lax.all_to_all(kv.reshape(grp * seq * head, rows, LANES), every, 0, 0, tiled=True)
    kv = kv.reshape(2, seq * head * rows, LANES)

    o_part, local = forward(lim, kv, x)
    local = [away(local, i) for i in range(chips)]
    o_part, stat = combine(o_part, local + [to_pair(p) for p in local])
    o_sum = lax.psum_scatter(o_part, "seq", scatter_dimension=0, tiled=False)
    d_kv, keep, send = backward(lim, kv, stat, x)
    got = to_pair(send)
    d_kv = lax.all_to_all(d_kv.reshape(grp * seq * head, rows, LANES), every, 0, 0, tiled=True)
    parts = [away(p, i) for i, p in enumerate(add_pair(lim, keep, got))]
    attended = join(lim, o_sum[0], to_other(o_sum[1]))
    parts, attended = lax.optimization_barrier((parts, attended))
    dq_own, dq_other = sum_parts(parts)
    dq_other = to_other(dq_other)
    d_states = encoder_grad(d_kv.reshape(2, seq, head, rows, LANES), w_key, w_value)
    dq_own, d_states = lax.optimization_barrier((dq_own, d_states))
    d_query = join(lim, dq_own, dq_other)
    return attended[None], d_query[None], d_states[None]


def solution(mesh):
    sizes = mesh.shape
    return jax.shard_map(
        functools.partial(on_device, sizes["grp"], sizes["seq"], sizes["head"]),
        mesh=mesh,
        in_specs=(
            P("grp", ("seq", "head"), None),
            P(),
            P(),
            P("grp", "seq", "head"),
            P("grp", "seq", "head"),
            P("grp"),
            P("grp"),
        ),
        out_specs=(
            P("grp", "seq", "head"),
            P("grp", "seq", "head"),
            P("grp", ("seq", "head"), None),
        ),
        check_vma=False,
    )
```
